128 devices in a mesh: gx: 32 (over y, x, core), gy: 4 (over z).
Axes of the slice: x: 4, y: 4, z: 4, core: 2. Of those that a mesh axis runs over, the one named last changes fastest.
Arguments:
- field: bfloat16 [64, 16, 64, 4096], P('gy', None, None, 'gx'), may hold values from -6 to 6
- conv_w: bfloat16 [27, 64, 64], replicated, may hold values from -0.15625 to 0.15625
- spec_re: float32 [16, 64, 64], replicated, may hold values from -6 to 6
- spec_im: float32 [16, 64, 64], replicated, may hold values from -6 to 6
- mlp_in: bfloat16 [256, 64], replicated, may hold values from -0.75 to 0.75
- mlp_out: bfloat16 [64, 256], replicated, may hold values from -0.375 to 0.375
Outputs:
- result: bfloat16 [64, 16, 64, 4096], P('gy', None, None, 'gx')
The draws below stay inside these ranges and needn't reach their ends.
All inputs are finite; a program needn't handle non-finite values.
Results may differ from the reference program's by a relative error of at most 0.0062.
Values may be sent and summed in bfloat16 or wider, within the bound.
No kernel may reach another device: no remote copies, remote signals or barrier semaphores. Data moves between devices by JAX's collectives and lax.ppermute only.
A program may use at most 128 MiB of HBM per device.

```python
import math
import jax
import jax.numpy as jnp
from jax import lax

C = 64
HID = 256
MODES = 16
NZ = 16
NX = 4096
NY = 64


def block_levels(rng, dims, shards, least, top_value):
    def one(axis_at, parts):
        heights = jax.random.uniform(jax.random.fold_in(jax.random.fold_in(rng, 6), axis_at), (parts,), jnp.float32, least / len(shards), top_value / len(shards))
        return jnp.repeat(jnp.exp(heights), dims[axis_at] // parts).reshape((-1,) + (1,) * (len(dims) - axis_at - 1))

    loudness = one(*shards[0])
    for cut in shards[1:]:
        loudness = loudness * one(*cut)
    return loudness


def scatter_about(rng, dims, deviation, reach, split=(), held_as=jnp.bfloat16):
    factor_of = block_levels(rng, dims, split, -0.22, 0.18) if split else 1.0
    array = jax.random.normal(rng, dims, jnp.float32) * deviation * factor_of
    return jnp.minimum(jnp.maximum(array, -reach), reach).astype(held_as)


def setup_inputs(seed: int = 0) -> dict:
    arg_keys = jax.random.split(jax.random.key(seed), 7)
    field = scatter_about(arg_keys[0], (NY, NZ, C, NX), 1.0, 6.0, ((0, 4), (3, 32)))
    conv_w = scatter_about(arg_keys[1], (27, C, C), (27 * C) ** -0.5, 0.15625)
    spec_re = scatter_about(arg_keys[2], (MODES, C, C), 1.0, 6.0, (), jnp.float32)
    spec_im = scatter_about(arg_keys[3], (MODES, C, C), 1.0, 6.0, (), jnp.float32)
    mlp_in = scatter_about(arg_keys[4], (HID, C), C ** -0.5, 0.75)
    mlp_out = scatter_about(arg_keys[5], (C, HID), HID ** -0.5, 0.375)
    return {"field": field, "conv_w": conv_w, "spec_re": spec_re, "spec_im": spec_im, "mlp_in": mlp_in, "mlp_out": mlp_out}


def forward_table(start, count, total, modes):
    places = start + jnp.arange(count, dtype=jnp.int32)
    orders = jnp.arange(modes, dtype=jnp.int32)
    phase = (places[:, None] * orders[None, :]) % total
    angle = phase.astype(jnp.float32) * (2.0 * math.pi / total)
    return jnp.concatenate([jnp.cos(angle), -jnp.sin(angle)], axis=1).astype(jnp.bfloat16)


def inverse_table(start, count, total, modes):
    places = start + jnp.arange(count, dtype=jnp.int32)
    orders = jnp.arange(modes, dtype=jnp.int32)
    phase = (orders[:, None] * places[None, :]) % total
    angle = phase.astype(jnp.float32) * (2.0 * math.pi / total)
    scales = jnp.where(orders == 0, 1.0, 2.0).astype(jnp.float32) / total
    return jnp.concatenate([jnp.cos(angle) * scales[:, None], -jnp.sin(angle) * scales[:, None]], axis=0)


def mix_modes(spectrum, spec_re, spec_im):
    modes = spec_re.shape[0]
    real_part = spectrum[..., :modes]
    imag_part = spectrum[..., modes:]
    highest = lax.Precision.HIGHEST
    out_real = jnp.einsum("koc,...ck->...ok", spec_re, real_part, precision=highest) - jnp.einsum("koc,...ck->...ok", spec_im, imag_part, precision=highest)
    out_imag = jnp.einsum("koc,...ck->...ok", spec_re, imag_part, precision=highest) + jnp.einsum("koc,...ck->...ok", spec_im, real_part, precision=highest)
    return jnp.concatenate([out_real, out_imag], axis=-1)


def lift(field, conv_w):
    depth = field.shape[1]
    width = field.shape[3]
    padded = jnp.pad(field, ((1, 1), (1, 1), (0, 0), (1, 1)))
    weights = conv_w.astype(jnp.float32)

    def one_row(row_index):
        slab = lax.dynamic_slice_in_dim(padded, row_index, 3, 0).astype(jnp.float32)
        total = lax.dynamic_index_in_dim(field, row_index, 0, keepdims=False).astype(jnp.float32)
        for shift_y in range(3):
            for shift_z in range(3):
                for shift_x in range(3):
                    tap_index = (shift_y * 3 + shift_z) * 3 + shift_x
                    window = slab[shift_y, shift_z:shift_z + depth, :, shift_x:shift_x + width]
                    total = total + jnp.einsum("oc,zcx->zox", weights[tap_index], window)
        return total.astype(jnp.bfloat16)

    return lax.map(one_row, jnp.arange(field.shape[0], dtype=jnp.int32))


def reference(field, conv_w, spec_re, spec_im, mlp_in, mlp_out):
    lifted = lift(field, conv_w)
    forward = forward_table(0, NX, NX, MODES)
    spectrum = jnp.dot(lifted, forward, preferred_element_type=jnp.float32)
    mixed = mix_modes(spectrum, spec_re, spec_im)
    inverse = inverse_table(0, NX, NX, MODES)
    first_w = mlp_in.astype(jnp.float32)
    second_w = mlp_out.astype(jnp.float32)

    def finish(row_index):
        mixed_row = lax.dynamic_index_in_dim(mixed, row_index, 0, keepdims=False)
        lifted_row = lax.dynamic_index_in_dim(lifted, row_index, 0, keepdims=False)
        branch = jnp.dot(mixed_row, inverse, precision=lax.Precision.HIGHEST)
        blended = (lifted_row.astype(jnp.float32) + branch).astype(jnp.bfloat16)
        hidden = jax.nn.gelu(jnp.einsum("hc,zcx->zhx", first_w, blended.astype(jnp.float32))).astype(jnp.bfloat16)
        down = jnp.einsum("ch,zhx->zcx", second_w, hidden.astype(jnp.float32))
        return (blended.astype(jnp.float32) + down).astype(jnp.bfloat16)

    return lax.map(finish, jnp.arange(NY, dtype=jnp.int32))
```

```python
import functools
import math

import jax
import jax.numpy as jnp
import numpy as np
from jax import lax
from jax.experimental import pallas as pl
from jax.experimental.pallas import tpu as pltpu
from jax.sharding import PartitionSpec as P

BF = jnp.bfloat16
F32 = jnp.float32
LANES = 128
CH = 64
ROWS = 1024
PADDED = ROWS + 2 * CH
MODES = 16
HID = 256
VMEM = pltpu.VMEM


def params(mib):
    return pltpu.CompilerParams(vmem_limit_bytes=mib * 2**20)


def cost(flops, read):
    return pl.CostEstimate(flops=int(flops), bytes_accessed=int(read), transcendentals=0)


def tables(blocks, width):
    total = blocks * width
    places = np.arange(-1, total + 1, dtype=np.int64)
    orders = np.arange(MODES, dtype=np.int64)
    phase = (places[:, None] * orders[None, :]) % total
    angle = phase.astype(np.float32) * np.float32(2.0 * math.pi / total)
    both = np.concatenate([np.cos(angle), -np.sin(angle)], axis=1).astype(np.float32)
    inside = both.copy()
    inside[0] = 0
    inside[-1] = 0
    forward = np.zeros((blocks, width, 3, 4, 2 * MODES), np.float32)
    inverse = np.zeros((blocks, 2 * MODES, width), np.float32)
    weight = np.where(orders == 0, 1.0, 2.0).astype(np.float32) / np.float32(total)
    weight = np.concatenate([weight, weight])
    for b in range(blocks):
        for d in range(3):
            first = b * width - d + 1 + 1
            forward[b, :, d, :, :] = inside[first : first + width][:, None, :]
        inverse[b] = (both[b * width + 1 : (b + 1) * width + 1] * weight).T
    forward = forward.reshape(blocks, width, 3 * 4 * 2 * MODES).astype(jnp.bfloat16)
    inverse = np.tile(inverse, (1, 4, 1))
    high = inverse.astype(jnp.bfloat16)
    low = (inverse - high.astype(np.float32)).astype(jnp.bfloat16)
    return forward, np.concatenate([high, low], axis=1)


def band_kernel(w_ref, o_ref):
    zero = jnp.zeros((CH, CH), BF)
    for a in range(3):
        for zo in range(2):
            for d in range(3):
                parts = []
                for zi in range(4):
                    b = zi - zo
                    parts.append(w_ref[(3 * a + b) * 3 + d] if 0 <= b <= 2 else zero)
                o_ref[a * 128 + zo * 64 : a * 128 + zo * 64 + 64, d * 256 : d * 256 + 256] = (
                    jnp.concatenate(parts, axis=1)
                )


def banded(conv_w):
    return pl.pallas_call(
        band_kernel, out_shape=jax.ShapeDtypeStruct((384, 768), BF), name="band"
    )(conv_w)


def one_hot(height, pairs):
    x = lax.broadcasted_iota(jnp.int32, (height, LANES), 0)
    lane = lax.broadcasted_iota(jnp.int32, (height, LANES), 1)
    hit = jnp.zeros((height, LANES), F32)
    for row, column in pairs:
        hit = jnp.where((x == row) & (lane == column), 1.0, hit)
    return hit.astype(BF)


def group_mask(height, group):
    lane = lax.broadcasted_iota(jnp.int32, (height, LANES), 1)
    return lane // 32 == group


def dft_kernel(f_ref, t_ref, g_ref, own_ref, e_ref, tab_ref):
    for g in range(4):
        for d in range(3):
            part = t_ref[:, d * 128 : d * 128 + 128]
            tab_ref[g * 128 : g * 128 + 128, d * 128 : d * 128 + 128] = jnp.where(
                group_mask(128, g), part, jnp.zeros_like(part)
            )
    for i in range(4):
        for g in range(4):
            y = 4 * g + i
            tab_ref[g * 128 : g * 128 + 128, 384:512] = one_hot(
                128, [(127, 2 * y + 2), (0, 2 * y + 1)]
            )

        @pl.loop(0, 4)
        def _(r):
            at = pl.ds(pl.multiple_of(r * 256, 256), 256)
            left = jnp.concatenate([f_ref[4 * g + i, at, :] for g in range(4)], axis=1)
            out = jnp.dot(left, tab_ref[...], preferred_element_type=F32)
            for d in range(3):
                g_ref[i, d, at, :] = out[:, d * 128 : d * 128 + 128].astype(BF)
            own_ref[i, at, :] = out[:, 128:256]
            edge = out[:, 384:512].astype(BF)
            if i == 0:
                e_ref[at, :] = edge
            else:
                e_ref[at, :] = e_ref[at, :] + edge


def dft(field, table):
    return pl.pallas_call(
        dft_kernel,
        out_shape=(
            jax.ShapeDtypeStruct((4, 3, ROWS, LANES), BF),
            jax.ShapeDtypeStruct((4, ROWS, LANES), F32),
            jax.ShapeDtypeStruct((ROWS, LANES), BF),
        ),
        scratch_shapes=[VMEM((512, 512), BF)],
        compiler_params=params(32),
        cost_estimate=cost(4e9, 4e6),
        name="dft",
    )(field, table)


def halo_kernel(top_ref, bottom_ref, t_ref, e_in_ref, gt_ref, gb_ref, e_ref):
    def columns(pairs, group):
        parts = []
        for d in range(3):
            part = t_ref[:, d * 128 : d * 128 + 128]
            parts.append(jnp.where(group_mask(128, group), part, jnp.zeros_like(part)))
        return jnp.concatenate(parts + [one_hot(128, pairs)], axis=1)

    above = columns([(127, 0), (0, 127)], 0)
    below = columns([(127, 34), (0, 33)], 3)

    @pl.loop(0, 4)
    def _(r):
        at = pl.ds(pl.multiple_of(r * 256, 256), 256)
        up = jnp.dot(top_ref[at, :], above, preferred_element_type=F32).astype(BF)
        down = jnp.dot(bottom_ref[at, :], below, preferred_element_type=F32).astype(BF)
        for d in range(3):
            gt_ref[d, at, :] = up[:, d * 128 : d * 128 + 128]
            gb_ref[d, at, :] = down[:, d * 128 : d * 128 + 128]
        e_ref[at, :] = e_in_ref[at, :] + up[:, 384:512] + down[:, 384:512]


def halo_modes(top, bottom, table, edges):
    return pl.pallas_call(
        halo_kernel,
        out_shape=(
            jax.ShapeDtypeStruct((3, ROWS, LANES), BF),
            jax.ShapeDtypeStruct((3, ROWS, LANES), BF),
            jax.ShapeDtypeStruct((ROWS, LANES), BF),
        ),
        compiler_params=params(32),
        cost_estimate=cost(1e9, 1e6),
        name="halo_modes",
    )(top, bottom, table, edges)


def clear(x_ref, a1_ref, a2_ref, rows):
    zero = jnp.zeros((CH, LANES), BF)
    for r in range(rows):
        for d in range(3):
            x_ref[r, d, 0:CH, :] = zero
            x_ref[r, d, CH + ROWS : PADDED, :] = zero

    @pl.loop(0, 8)
    def _(g):
        at = pl.ds(pl.multiple_of(g * 128, 128), 128)
        a1_ref[at, :] = jnp.zeros((128, 256), F32)
        a2_ref[at, :] = jnp.zeros((128, 256), F32)


def band_conv(w_ref, x_ref, a1_ref, a2_ref, s_ref, half, emit, after):
    @pl.loop(0, half)
    def _(p):
        for g in range(8):
            r0 = g * 128
            at = slice(r0, r0 + 128)
            cells = jnp.concatenate(
                [
                    x_ref[p, :, r0 : r0 + 256, :].reshape(768, LANES),
                    x_ref[p + half, :, r0 : r0 + 256, :].reshape(768, LANES),
                ],
                axis=1,
            )
            part = jnp.dot(w_ref[...], cells, preferred_element_type=F32)
            done = a2_ref[at, :] + part[256:384]
            a2_ref[at, :] = a1_ref[at, :] + part[128:256]
            a1_ref[at, :] = part[0:128]
            emit(jnp.maximum(p - 2, 0), at, done[:, 0:128])
            emit(p + half - 2, at, done[:, 128:256])
            s_ref[jnp.minimum(p, 2), at, :] = done[:, 128:256]
            after(p, r0)

    for g in range(8):
        at = slice(g * 128, g * 128 + 128)
        emit(half - 2, at, a2_ref[at, 0:128] + s_ref[0, at, :])
        emit(half - 1, at, a1_ref[at, 0:128] + s_ref[1, at, :])


def spectral_kernel(w_ref, g_ref, own_ref, gt_ref, gb_ref, o_ref, x_ref, a1_ref, a2_ref, s_ref):
    clear(x_ref, a1_ref, a2_ref, 6)
    lane = lax.broadcasted_iota(jnp.int32, (256, LANES), 1)
    for r0 in range(0, ROWS, 256):
        src, dst = slice(r0, r0 + 256), slice(CH + r0, CH + r0 + 256)
        for d in range(3):
            for i in range(4):
                x_ref[i + 1, d, dst, :] = g_ref[i, d, src, :]
            x_ref[0, d, dst, :] = jnp.where(
                lane < 32, gt_ref[d, src, :], pltpu.roll(g_ref[3, d, src, :], 32, 1)
            )
            x_ref[5, d, dst, :] = jnp.where(
                lane >= 96, gb_ref[d, src, :], pltpu.roll(g_ref[0, d, src, :], 96, 1)
            )

    def emit(row, at, value):
        o_ref[row, at, :] = (value + own_ref[row, at, :]).astype(BF)

    band_conv(w_ref, x_ref, a1_ref, a2_ref, s_ref, 3, emit, lambda p, r0: None)


def conv_scratch(rows):
    return [
        VMEM((rows, 3, PADDED, LANES), BF),
        VMEM((ROWS, 256), F32),
        VMEM((ROWS, 256), F32),
        VMEM((3, ROWS, LANES), F32),
    ]


def spectral(band, modes, own, above, below):
    return pl.pallas_call(
        spectral_kernel,
        out_shape=jax.ShapeDtypeStruct((4, ROWS, LANES), BF),
        scratch_shapes=conv_scratch(6),
        compiler_params=params(48),
        cost_estimate=cost(4e9, 8e6),
        name="spectral",
    )(band, modes, own, above, below)


def lift_kernel(part, w_ref, f_ref, halo_ref, el_ref, er_ref, *rest):
    o_ref, x_ref, a1_ref, a2_ref, s_ref, ed_ref = rest[-6:]
    half = 5
    first = 8 * part
    clear(x_ref, a1_ref, a2_ref, 2 * half)
    lane = lax.broadcasted_iota(jnp.int32, (128, LANES), 1)
    halo_at = 0 if part == 0 else 9
    body = slice(CH, CH + ROWS)
    for r in range(10):
        if r == halo_at:
            x_ref[r, 1, body, :] = halo_ref[...]
        else:
            x_ref[r, 1, body, :] = f_ref[first + r - 1]
    for r0 in range(0, ROWS, 128):
        at = slice(r0, r0 + 128)
        ed_ref[at, :] = jnp.where(lane % 2 == 0, el_ref[at, :], er_ref[at, :])

    def build(r, r0):
        at = slice(CH + r0, CH + r0 + 128)
        mid = x_ref[r, 1, at, :]
        edge = pltpu.roll(ed_ref[r0 : r0 + 128, :], 128 - 2 * (first + r), 1)
        x_ref[r, 0, at, :] = jnp.where(lane == 0, edge, pltpu.roll(mid, 1, 1))
        x_ref[r, 2, at, :] = jnp.where(lane == 127, edge, pltpu.roll(mid, 127, 1))

    for r0 in range(0, ROWS, 128):
        build(0, r0)
        build(half, r0)

    def after(p, r0):
        later = jnp.minimum(p + 1, half - 1)
        build(later, r0)
        build(later + half, r0)

    def emit(row, at, value):
        same = x_ref[row + 1, 1, CH + at.start : CH + at.stop, :].astype(F32)
        o_ref[row, at, :] = (value + same).astype(BF)

    band_conv(w_ref, x_ref, a1_ref, a2_ref, s_ref, half, emit, after)


def lift(part, band, field, halo, left, right, into=None):
    whole = pl.BlockSpec(memory_space=VMEM)
    operands = [band, field, halo, left, right]
    specs = [whole] * 5
    aliases = {}
    if into is not None:
        operands.append(into)
        specs.append(pl.BlockSpec(memory_space=pl.ANY))
        aliases = {5: 0}
    return pl.pallas_call(
        functools.partial(lift_kernel, part),
        grid=(1,),
        in_specs=specs,
        out_specs=pl.BlockSpec((8, ROWS, LANES), lambda i: (part, 0, 0)),
        out_shape=jax.ShapeDtypeStruct((16, ROWS, LANES), BF),
        scratch_shapes=conv_scratch(10) + [VMEM((ROWS, LANES), BF)],
        input_output_aliases=aliases,
        compiler_params=params(48),
        cost_estimate=cost(8e9, 8e6),
        name="lift",
    )(*operands)


def split(x):
    high = x.astype(BF)
    return high, (x - high.astype(F32)).astype(BF)


def mix_kernel(p_ref, re_ref, im_ref, o_ref):
    total = p_ref[0].astype(F32)
    for i in range(1, 16):
        total = total + p_ref[i].astype(F32)
    both = jnp.concatenate([total[0:CH], total[CH : 2 * CH]], axis=1)
    lane = lax.broadcasted_iota(jnp.int32, (CH, 256), 1)
    is_re = lane % 32 < MODES
    turned = jnp.where(is_re, -pltpu.roll(both, 256 - MODES, 1), pltpu.roll(both, MODES, 1))
    bh, bl = split(both)
    th, tl = split(turned)
    mode = lane % MODES
    out = jnp.zeros((CH, 256), F32)
    for k in range(MODES):
        rh, rl = split(re_ref[k])
        ih, il = split(im_ref[k])
        dot = functools.partial(jnp.dot, preferred_element_type=F32)
        one = dot(rh, bh) + dot(ih, th) + (dot(rl, bh) + dot(il, th)) + (dot(rh, bl) + dot(ih, tl))
        out = jnp.where(mode == k, one, out)
    piece = jnp.concatenate([out[:, 0:128], out[:, 128:256]], axis=0).astype(BF)
    for i in range(16):
        o_ref[i] = piece


def mix(pieces, spec_re, spec_im):
    return pl.pallas_call(
        mix_kernel,
        out_shape=jax.ShapeDtypeStruct((16, 128, LANES), BF),
        compiler_params=params(16),
        cost_estimate=cost(5e8, 1e6),
        name="mix",
    )(pieces, spec_re, spec_im)


def finish_kernel(h_ref, l_ref, m_ref, inv_ref, up_ref, down_ref, o_ref, tab_ref):
    step = pl.program_id(0)
    ii = step % 2

    row = lax.broadcasted_iota(jnp.int32, (256, LANES), 0)
    inv = inv_ref[...]
    tab_ref[...] = jnp.where((row // 32) % 4 == step // 2, inv, jnp.zeros_like(inv))

    @pl.loop(0, 4)
    def _(q):
        at = pl.ds(pl.multiple_of(q * 256, 256), 256)
        m = m_ref[ii, at, :]
        branch = jnp.dot(
            jnp.concatenate([m, m], axis=1), tab_ref[...], preferred_element_type=F32
        )
        blended = (l_ref[0, at, :].astype(F32) + branch).astype(BF)
        outs = []
        for z in range(0, 4, 2):
            pair = jnp.concatenate(
                [blended[z * 64 : z * 64 + 64], blended[z * 64 + 64 : z * 64 + 128]], axis=1
            )
            hidden = jax.nn.gelu(
                jnp.dot(up_ref[...], pair, preferred_element_type=F32)
            ).astype(BF)
            out = pair.astype(F32) + jnp.dot(
                down_ref[...], hidden, preferred_element_type=F32
            )
            outs += [out[:, 0:128], out[:, 128:256]]
        o_ref[0, at, :] = jnp.concatenate(outs, axis=0).astype(BF)


def finish(which, lifted, mixed, inverse, mlp_in, mlp_out):
    layer = lambda s, h: (4 * (s // 2) + 2 * h[0] + s % 2, 0, 0)
    fixed = lambda *shape: pl.BlockSpec(shape, lambda s, h: (0,) * len(shape))
    return pl.pallas_call(
        finish_kernel,
        grid_spec=pltpu.PrefetchScalarGridSpec(
            num_scalar_prefetch=1,
            grid=(8,),
            in_specs=[
                pl.BlockSpec((1, ROWS, LANES), layer),
                fixed(2, ROWS, LANES),
                fixed(256, LANES),
                fixed(HID, CH),
                fixed(CH, HID),
            ],
            out_specs=pl.BlockSpec((1, ROWS, LANES), layer),
            scratch_shapes=[VMEM((256, LANES), BF)],
        ),
        out_shape=jax.ShapeDtypeStruct((16, ROWS, LANES), BF),
        input_output_aliases={1: 0},
        compiler_params=params(32),
        cost_estimate=cost(5e9, 6e6),
        name="finish",
    )(which, lifted, mixed, inverse, mlp_in, mlp_out)


def per_device(forward, inverse, field, conv_w, spec_re, spec_im, mlp_in, mlp_out):
    rows_y, depth, channels, width = field.shape
    blocks, layers = lax.axis_size("gx"), lax.axis_size("gy")
    place = lax.axis_index("gx")
    core = place % 2
    f = field.reshape(rows_y, depth * channels, width)

    up_y = [(i, i + 1) for i in range(layers - 1)]
    down_y = [(j, i) for i, j in up_y]
    up_x = [(i, i + 1) for i in range(blocks - 1)]
    down_x = [(j, i) for i, j in up_x]
    partner = [(i, i ^ 1) for i in range(blocks)]
    chips = [[i for i in range(c, blocks, 2)] for c in range(2)]

    top = lax.ppermute(f[rows_y - 1], "gy", up_y)
    bottom = lax.ppermute(f[0], "gy", down_y)
    table = lax.dynamic_index_in_dim(forward, place, 0, keepdims=False)
    inv = lax.dynamic_index_in_dim(inverse, place, 0, keepdims=False)
    band = banded(conv_w)

    modes, own, edges = dft(f, table)
    above, below, edges = halo_modes(top, bottom, table, edges)
    left = lax.ppermute(edges, "gx", up_x)
    right = lax.ppermute(edges, "gx", down_x)

    part = spectral(band, modes, own, above, below)
    mine = lax.dynamic_slice_in_dim(part, 2 * core, 2, 0)
    other = lax.dynamic_slice_in_dim(part, 2 - 2 * core, 2, 0)
    theirs = lax.ppermute(other, "gx", partner)
    chip_sum = (mine.astype(F32) + theirs.astype(F32)).astype(BF)
    pieces = lax.all_to_all(
        chip_sum.reshape(16, 128, LANES), "gx", 0, 0, axis_index_groups=chips, tiled=True
    )
    lifted = lift(0, band, f, top, left, right)
    copies = mix(pieces, spec_re, spec_im)
    mixed = lax.all_to_all(copies, "gx", 0, 0, axis_index_groups=chips, tiled=True)
    lifted = lift(1, band, f, bottom, left, right, lifted)
    mixed = mixed.reshape(2, ROWS, LANES)
    mixed_other = lax.ppermute(mixed, "gx", partner)
    which = core[None].astype(jnp.int32)
    result = finish(which, lifted, mixed, inv, mlp_in, mlp_out)
    result = finish(1 - which, result, mixed_other, inv, mlp_in, mlp_out)
    return result.reshape(field.shape)


def solution(mesh):
    in_specs = (P("gy", None, None, "gx"), P(), P(), P(), P(), P())
    out_specs = P("gy", None, None, "gx")
    forward, inverse = tables(mesh.shape["gx"], LANES)
    return jax.shard_map(
        functools.partial(per_device, jnp.asarray(forward), jnp.asarray(inverse)),
        mesh=mesh, in_specs=in_specs, out_specs=out_specs, check_vma=False,
    )
```

```python
import functools
import math

import jax
import jax.numpy as jnp
import numpy as np
from jax import lax
from jax.experimental import pallas as pl
from jax.experimental.pallas import tpu as pltpu
from jax.sharding import PartitionSpec as P

BF = jnp.bfloat16
F32 = jnp.float32
LANES = 128
CH = 64
ROWS = 1024
PADDED = ROWS + 2 * CH
MODES = 16
HID = 256
CHUNK = 512
BATCH = 1
DFT_MIB = 46
VMEM = pltpu.VMEM


def params(mib):
    return pltpu.CompilerParams(vmem_limit_bytes=mib * 2**20)


def cost(flops, read):
    return pl.CostEstimate(flops=int(flops), bytes_accessed=int(read), transcendentals=0)


def tables(blocks, width):
    total = blocks * width
    places = np.arange(-1, total + 1, dtype=np.int64)
    orders = np.arange(MODES, dtype=np.int64)
    phase = (places[:, None] * orders[None, :]) % total
    angle = phase.astype(np.float32) * np.float32(2.0 * math.pi / total)
    both = np.concatenate([np.cos(angle), -np.sin(angle)], axis=1).astype(np.float32)
    inside = both.copy()
    inside[0] = 0
    inside[-1] = 0
    forward = np.zeros((blocks, width, 3, 4, 2 * MODES), np.float32)
    inverse = np.zeros((blocks, 2 * MODES, width), np.float32)
    weight = np.where(orders == 0, 1.0, 2.0).astype(np.float32) / np.float32(total)
    weight = np.concatenate([weight, weight])
    for b in range(blocks):
        for d in range(3):
            first = b * width - d + 1 + 1
            forward[b, :, d, :, :] = inside[first : first + width][:, None, :]
        inverse[b] = (both[b * width + 1 : (b + 1) * width + 1] * weight).T
    forward = forward.reshape(blocks, width, 3 * 4 * 2 * MODES).astype(jnp.bfloat16)
    inverse = np.tile(inverse, (1, 4, 1))
    high = inverse.astype(jnp.bfloat16)
    low = (inverse - high.astype(np.float32)).astype(jnp.bfloat16)
    return forward, np.concatenate([high, low], axis=1)


def band_kernel(w_ref, o_ref):
    zero = jnp.zeros((CH, CH), BF)
    for a in range(3):
        for zo in range(2):
            for d in range(3):
                parts = []
                for zi in range(4):
                    b = zi - zo
                    parts.append(w_ref[(3 * a + b) * 3 + d] if 0 <= b <= 2 else zero)
                o_ref[a * 128 + zo * 64 : a * 128 + zo * 64 + 64, d * 256 : d * 256 + 256] = (
                    jnp.concatenate(parts, axis=1)
                )


def banded(conv_w):
    return pl.pallas_call(
        band_kernel, out_shape=jax.ShapeDtypeStruct((384, 768), BF), name="band"
    )(conv_w)


def one_hot(height, pairs):
    x = lax.broadcasted_iota(jnp.int32, (height, LANES), 0)
    lane = lax.broadcasted_iota(jnp.int32, (height, LANES), 1)
    hit = jnp.zeros((height, LANES), F32)
    for row, column in pairs:
        hit = jnp.where((x == row) & (lane == column), 1.0, hit)
    return hit.astype(BF)


def group_mask(height, group):
    lane = lax.broadcasted_iota(jnp.int32, (height, LANES), 1)
    return lane // 32 == group


def dft_kernel(f_ref, t_ref, g_ref, own_ref, e_ref, tab_ref, f_buf, sem):
    fetch = [pltpu.make_async_copy(f_ref.at[y], f_buf.at[y], sem.at[y]) for y in range(16)]
    for i in range(4):
        for g in range(4):
            fetch[4 * g + i].start()
    for g in range(4):
        for d in range(3):
            part = t_ref[:, d * 128 : d * 128 + 128]
            tab_ref[g * 128 : g * 128 + 128, d * 128 : d * 128 + 128] = jnp.where(
                group_mask(128, g), part, jnp.zeros_like(part)
            )
    for i in range(4):
        for g in range(4):
            y = 4 * g + i
            tab_ref[g * 128 : g * 128 + 128, 384:512] = one_hot(
                128, [(127, 2 * y + 2), (0, 2 * y + 1)]
            )
        for g in range(4):
            fetch[4 * g + i].wait()

        @pl.loop(0, ROWS // CHUNK)
        def _(r):
            at = pl.ds(pl.multiple_of(r * CHUNK, CHUNK), CHUNK)
            left = jnp.concatenate([f_buf[4 * g + i, at, :] for g in range(4)], axis=1)
            out = jnp.dot(left, tab_ref[...], preferred_element_type=F32)
            for d in range(3):
                g_ref[i, d, at, :] = out[:, d * 128 : d * 128 + 128].astype(BF)
            own_ref[i, at, :] = out[:, 128:256]
            edge = out[:, 384:512].astype(BF)
            if i == 0:
                e_ref[at, :] = edge
            else:
                e_ref[at, :] = e_ref[at, :] + edge


def dft(field, table):
    return pl.pallas_call(
        dft_kernel,
        in_specs=[pl.BlockSpec(memory_space=pltpu.HBM), pl.BlockSpec(memory_space=VMEM)],
        out_shape=(
            jax.ShapeDtypeStruct((4, 3, ROWS, LANES), BF),
            jax.ShapeDtypeStruct((4, ROWS, LANES), F32),
            jax.ShapeDtypeStruct((ROWS, LANES), BF),
        ),
        scratch_shapes=[
            VMEM((512, 512), BF),
            VMEM((16, ROWS, LANES), BF),
            pltpu.SemaphoreType.DMA((16,)),
        ],
        compiler_params=params(DFT_MIB),
        cost_estimate=cost(4e9, 4e6),
        name="dft",
    )(field, table)


def halo_kernel(top_ref, bottom_ref, t_ref, e_in_ref, gt_ref, gb_ref, e_ref):
    def columns(pairs, group):
        parts = []
        for d in range(3):
            part = t_ref[:, d * 128 : d * 128 + 128]
            parts.append(jnp.where(group_mask(128, group), part, jnp.zeros_like(part)))
        return jnp.concatenate(parts + [one_hot(128, pairs)], axis=1)

    above = columns([(127, 0), (0, 127)], 0)
    below = columns([(127, 34), (0, 33)], 3)

    @pl.loop(0, ROWS // CHUNK)
    def _(r):
        at = pl.ds(pl.multiple_of(r * CHUNK, CHUNK), CHUNK)
        up = jnp.dot(top_ref[at, :], above, preferred_element_type=F32).astype(BF)
        down = jnp.dot(bottom_ref[at, :], below, preferred_element_type=F32).astype(BF)
        for d in range(3):
            gt_ref[d, at, :] = up[:, d * 128 : d * 128 + 128]
            gb_ref[d, at, :] = down[:, d * 128 : d * 128 + 128]
        e_ref[at, :] = e_in_ref[at, :] + up[:, 384:512] + down[:, 384:512]


def halo_modes(top, bottom, table, edges):
    return pl.pallas_call(
        halo_kernel,
        out_shape=(
            jax.ShapeDtypeStruct((3, ROWS, LANES), BF),
            jax.ShapeDtypeStruct((3, ROWS, LANES), BF),
            jax.ShapeDtypeStruct((ROWS, LANES), BF),
        ),
        compiler_params=params(32),
        cost_estimate=cost(1e9, 1e6),
        name="halo_modes",
    )(top, bottom, table, edges)


def clear(x_ref, a1_ref, a2_ref, rows):
    zero = jnp.zeros((CH, LANES), BF)
    for r in range(rows):
        for d in range(3):
            x_ref[r, d, 0:CH, :] = zero
            x_ref[r, d, CH + ROWS : PADDED, :] = zero

    @pl.loop(0, 8)
    def _(g):
        at = pl.ds(pl.multiple_of(g * 128, 128), 128)
        a1_ref[at, :] = jnp.zeros((128, 256), F32)
        a2_ref[at, :] = jnp.zeros((128, 256), F32)


def band_conv(w_ref, x_ref, a1_ref, a2_ref, s_ref, half, emit, before, after):
    @pl.loop(0, half)
    def _(p):
        before(p)
        for g0 in range(0, 8, BATCH):
            cells = []
            for g in range(g0, g0 + BATCH):
                for layer in (p, p + half):
                    rows = x_ref[layer, :, g * 128 : g * 128 + 256, :]
                    cells.append(rows.reshape(768, LANES))
            parts = jnp.dot(
                w_ref[...], jnp.concatenate(cells, axis=1), preferred_element_type=F32
            )
            for g in range(g0, g0 + BATCH):
                at = slice(g * 128, g * 128 + 128)
                part = parts[:, (g - g0) * 256 : (g - g0) * 256 + 256]
                done = a2_ref[at, :] + part[256:384]
                a2_ref[at, :] = a1_ref[at, :] + part[128:256]
                a1_ref[at, :] = part[0:128]
                emit(jnp.maximum(p - 2, 0), at, done[:, 0:128])
                emit(p + half - 2, at, done[:, 128:256])
                s_ref[jnp.minimum(p, 2), at, :] = done[:, 128:256]
                after(p, g * 128)

    for g in range(8):
        at = slice(g * 128, g * 128 + 128)
        emit(half - 2, at, a2_ref[at, 0:128] + s_ref[0, at, :])
        emit(half - 1, at, a1_ref[at, 0:128] + s_ref[1, at, :])


def conv_scratch(rows):
    return [
        VMEM((rows, 3, PADDED, LANES), BF),
        VMEM((ROWS, 256), F32),
        VMEM((ROWS, 256), F32),
        VMEM((3, ROWS, LANES), F32),
    ]


def spectral_kernel(
    at_ref, w_ref, g_ref, own_ref, gt_ref, gb_ref, mine_ref, other_ref,
    x_ref, a1_ref, a2_ref, s_ref, o_ref
):
    clear(x_ref, a1_ref, a2_ref, 6)
    lane = lax.broadcasted_iota(jnp.int32, (256, LANES), 1)
    for r0 in range(0, ROWS, 256):
        src, dst = slice(r0, r0 + 256), slice(CH + r0, CH + r0 + 256)
        for d in range(3):
            for i in range(4):
                x_ref[i + 1, d, dst, :] = g_ref[i, d, src, :]
            x_ref[0, d, dst, :] = jnp.where(
                lane < 32, gt_ref[d, src, :], pltpu.roll(g_ref[3, d, src, :], 32, 1)
            )
            x_ref[5, d, dst, :] = jnp.where(
                lane >= 96, gb_ref[d, src, :], pltpu.roll(g_ref[0, d, src, :], 96, 1)
            )
    shift = 2 * at_ref[0]

    def emit(row, at, value):
        o_ref[(row + shift) % 4, at, :] = (value + own_ref[row, at, :]).astype(BF)

    band_conv(w_ref, x_ref, a1_ref, a2_ref, s_ref, 3, emit, lambda p: None, lambda p, r0: None)
    mine_ref[...] = o_ref[0:2]
    other_ref[...] = o_ref[2:4]


def spectral(where, band, modes, own, above, below):
    half = jax.ShapeDtypeStruct((2, ROWS, LANES), BF)
    return pl.pallas_call(
        spectral_kernel,
        in_specs=[pl.BlockSpec(memory_space=pltpu.SMEM)] + [pl.BlockSpec(memory_space=VMEM)] * 5,
        out_shape=(half, half),
        scratch_shapes=conv_scratch(6) + [VMEM((4, ROWS, LANES), BF)],
        compiler_params=params(40),
        cost_estimate=cost(4e9, 8e6),
        name="spectral",
    )(where, band, modes, own, above, below)


def add_kernel(a_ref, b_ref, o_ref):
    o_ref[...] = (a_ref[...].astype(F32) + b_ref[...].astype(F32)).astype(BF)


def add(a, b):
    return pl.pallas_call(
        add_kernel,
        out_shape=jax.ShapeDtypeStruct(a.shape, BF),
        compiler_params=params(16),
        cost_estimate=cost(1e6, 2e6),
        name="add",
    )(a, b)


def lift_kernel(
    part, w_ref, f_ref, halo_ref, el_ref, er_ref, o_ref,
    w_buf, x_ref, a1_ref, a2_ref, s_ref, ed_ref, o_buf, sem, in_sem, out_sem
):
    half = 5
    first = 8 * part
    body = slice(CH, CH + ROWS)
    edges = [
        pltpu.make_async_copy(el_ref, ed_ref.at[0], in_sem.at[0]),
        pltpu.make_async_copy(er_ref, ed_ref.at[1], in_sem.at[1]),
    ]
    weights = pltpu.make_async_copy(w_ref, w_buf, in_sem.at[2])
    fetch = []
    for r in range(10):
        src = halo_ref if first + r in (0, 17) else f_ref.at[first + r - 1]
        fetch.append(pltpu.make_async_copy(src, x_ref.at[r, 1, body, :], sem.at[r]))
    later = [r + k for r in range(1, half) for k in (0, half) if r + k != half - 1]
    for copy in edges + [fetch[0], fetch[half], weights, fetch[half - 1]]:
        copy.start()
    for r in later:
        fetch[r].start()
    clear(x_ref, a1_ref, a2_ref, 2 * half)
    lane = lax.broadcasted_iota(jnp.int32, (128, LANES), 1)
    for copy in edges:
        copy.wait()
    for r0 in range(0, ROWS, 128):
        at = slice(r0, r0 + 128)
        ed_ref[0, at, :] = jnp.where(lane % 2 == 0, ed_ref[0, at, :], ed_ref[1, at, :])

    def build(r, r0):
        at = slice(CH + r0, CH + r0 + 128)
        mid = x_ref[r, 1, at, :]
        edge = pltpu.roll(ed_ref[0, r0 : r0 + 128, :], 128 - 2 * (first + r), 1)
        x_ref[r, 0, at, :] = jnp.where(lane == 0, edge, pltpu.roll(mid, 1, 1))
        x_ref[r, 2, at, :] = jnp.where(lane == 127, edge, pltpu.roll(mid, 127, 1))

    fetch[0].wait()
    fetch[half].wait()
    for r0 in range(0, ROWS, 128):
        build(0, r0)
        build(half, r0)
    weights.wait()
    fetch[half - 1].wait()

    def arrived(r):
        pltpu.make_async_copy(halo_ref, x_ref.at[r, 1, body, :], sem.at[r]).wait()

    def out(row):
        return pltpu.make_async_copy(o_buf.at[row], o_ref.at[row], out_sem.at[row])

    def before(p):
        @pl.when(p < half - 2)
        def _():
            arrived(p + 1)

        @pl.when(p < half - 1)
        def _():
            arrived(p + 1 + half)

        @pl.when(p > 2)
        def _():
            out(p - 3).start()
            out(p + half - 3).start()

    def after(p, r0):
        following = jnp.minimum(p + 1, half - 1)
        build(following, r0)
        build(following + half, r0)

    def emit(row, at, value):
        same = x_ref[row + 1, 1, CH + at.start : CH + at.stop, :].astype(F32)
        o_buf[row, at, :] = (value + same).astype(BF)

    band_conv(w_buf, x_ref, a1_ref, a2_ref, s_ref, half, emit, before, after)
    for row in (half - 3, 2 * half - 3, half - 2, half - 1):
        out(row).start()
    for row in range(8):
        out(row).wait()


def lift(part, band, field, halo, left, right):
    anywhere = pl.BlockSpec(memory_space=pl.ANY)
    return pl.pallas_call(
        functools.partial(lift_kernel, part),
        in_specs=[anywhere] * 5,
        out_specs=anywhere,
        out_shape=jax.ShapeDtypeStruct((8, ROWS, LANES), BF),
        scratch_shapes=[VMEM((384, 768), BF)]
        + conv_scratch(10)
        + [
            VMEM((2, ROWS, LANES), BF),
            VMEM((8, ROWS, LANES), BF),
            pltpu.SemaphoreType.DMA((10,)),
            pltpu.SemaphoreType.DMA((3,)),
            pltpu.SemaphoreType.DMA((8,)),
        ],
        compiler_params=params(60),
        cost_estimate=cost(8e9, 8e6),
        name="lift",
    )(band, field, halo, left, right)


def split(x):
    high = x.astype(BF)
    return high, (x - high.astype(F32)).astype(BF)


def mix_kernel(p_ref, re_ref, im_ref, o_ref):
    total = p_ref[0].astype(F32)
    for i in range(1, 16):
        total = total + p_ref[i].astype(F32)
    both = jnp.concatenate([total[0:CH], total[CH : 2 * CH]], axis=1)
    lane = lax.broadcasted_iota(jnp.int32, (CH, 256), 1)
    is_re = lane % 32 < MODES
    turned = jnp.where(is_re, -pltpu.roll(both, 256 - MODES, 1), pltpu.roll(both, MODES, 1))
    bh, bl = split(both)
    th, tl = split(turned)
    dot = functools.partial(jnp.dot, preferred_element_type=F32)
    rh, rl = split(re_ref[...].reshape(MODES * CH, CH))
    ih, il = split(im_ref[...].reshape(MODES * CH, CH))
    high = jnp.concatenate([rh, ih], axis=1)
    low = jnp.concatenate([rl, il], axis=1)
    cells = jnp.concatenate([bh, th], axis=0)
    rest = jnp.concatenate([bl, tl], axis=0)
    every = dot(
        jnp.concatenate([high, low], axis=1), jnp.concatenate([cells, cells], axis=0)
    ) + dot(high, rest)
    mode = lane % MODES
    out = every[0:CH]
    for k in range(1, MODES):
        out = jnp.where(mode == k, every[k * CH : k * CH + CH], out)
    piece = jnp.concatenate([out[:, 0:128], out[:, 128:256]], axis=0).astype(BF)
    for i in range(16):
        o_ref[i] = piece


def mix(pieces, spec_re, spec_im):
    return pl.pallas_call(
        mix_kernel,
        out_shape=jax.ShapeDtypeStruct((16, 128, LANES), BF),
        compiler_params=params(16),
        cost_estimate=cost(5e8, 1e6),
        name="mix",
    )(pieces, spec_re, spec_im)


GELU_ONE = math.sqrt(2.0 / math.pi)
GELU_THREE = GELU_ONE * 0.044715


def finish_kernel(h_ref, la_ref, lb_ref, m_ref, inv_ref, up_ref, down_ref, *rest):
    o_ref, tab_ref = rest[-2:]

    @pl.when(pl.program_id(0) == 0)
    def _():
        row = lax.broadcasted_iota(jnp.int32, (256, LANES), 0)
        inv = inv_ref[0]
        for g in range(4):
            tab_ref[:, g * 128 : g * 128 + 128] = jnp.where(
                (row // 32) % 4 == g, inv, jnp.zeros_like(inv)
            )

    dot = functools.partial(jnp.dot, preferred_element_type=F32)
    m = m_ref[0]
    branch = dot(jnp.concatenate([m, m], axis=1), tab_ref[...])
    lifted = jnp.concatenate([ref[g, 0] for ref in (la_ref, lb_ref) for g in range(2)], axis=1)
    blended = (lifted.astype(F32) + branch).astype(BF)
    cells = jnp.concatenate(
        [blended[z * CH : z * CH + CH] for z in range(CHUNK // CH)], axis=1
    )
    x = dot(up_ref[...], cells)
    bend = jnp.tanh(x * (GELU_ONE + GELU_THREE * (x * x)))
    hidden = (0.5 * x * bend + 0.5 * x).astype(BF)
    out = cells.astype(F32) + dot(down_ref[...], hidden)
    for z in range(CHUNK // CH):
        for g in range(4):
            c = (z * 4 + g) * 128
            o_ref[g, 0, z * CH : z * CH + CH, :] = out[:, c : c + 128].astype(BF)


def finish(half_at, where, first, last, mixed, inverse, mlp_in, mlp_out, into=None):
    chunks = ROWS // CHUNK
    layer = lambda s, h: (0, 2 * h[half_at] + s // chunks, s % chunks, 0)
    fixed = lambda *shape: pl.BlockSpec(shape, lambda s, h: (0,) * len(shape))
    operands = [where, first, last, mixed, inverse, mlp_in, mlp_out]
    specs = [
        pl.BlockSpec((2, 1, CHUNK, LANES), layer),
        pl.BlockSpec((2, 1, CHUNK, LANES), layer),
        pl.BlockSpec((1, CHUNK, LANES), lambda s, h: (s // chunks, s % chunks, 0)),
        pl.BlockSpec((1, 256, LANES), lambda s, h: (h[1], 0, 0)),
        fixed(HID, CH),
        fixed(CH, HID),
    ]
    if into is not None:
        operands.append(into)
        specs.append(pl.BlockSpec(memory_space=pltpu.HBM))
    return pl.pallas_call(
        finish_kernel,
        grid_spec=pltpu.PrefetchScalarGridSpec(
            num_scalar_prefetch=1,
            grid=(2 * chunks,),
            in_specs=specs,
            out_specs=pl.BlockSpec((4, 1, CHUNK, LANES), layer),
            scratch_shapes=[VMEM((256, 512), BF)],
        ),
        out_shape=jax.ShapeDtypeStruct((4, 4, ROWS, LANES), BF),
        input_output_aliases={} if into is None else {7: 0},
        compiler_params=params(58),
        cost_estimate=cost(5e9, 6e6),
        name="finish",
    )(*operands)


def per_device(forward, inverse, field, conv_w, spec_re, spec_im, mlp_in, mlp_out):
    rows_y, depth, channels, width = field.shape
    blocks, layers = lax.axis_size("gx"), lax.axis_size("gy")
    place = lax.axis_index("gx")
    core = place % 2
    f = field.reshape(rows_y, depth * channels, width)

    up_y = [(i, i + 1) for i in range(layers - 1)]
    down_y = [(j, i) for i, j in up_y]
    up_x = [(i, i + 1) for i in range(blocks - 1)]
    down_x = [(j, i) for i, j in up_x]
    partner = [(i, i ^ 1) for i in range(blocks)]
    chips = [[i for i in range(c, blocks, 2)] for c in range(2)]

    top = lax.ppermute(f[rows_y - 1], "gy", up_y)
    bottom = lax.ppermute(f[0], "gy", down_y)
    band = banded(conv_w)
    where = jnp.stack([core, place, 1 - core]).astype(jnp.int32)
    table = lax.dynamic_index_in_dim(forward, place, 0, keepdims=False)
    modes, own, edges = dft(f, table)
    above, below, edges = halo_modes(top, bottom, table, edges)
    left = lax.ppermute(edges, "gx", up_x)
    right = lax.ppermute(edges, "gx", down_x)
    mine, other = spectral(where, band, modes, own, above, below)
    other, left, right = lax.optimization_barrier((other, left, right))
    theirs = lax.ppermute(other, "gx", partner)
    chip_sum = add(mine, theirs)
    pieces = lax.all_to_all(
        chip_sum.reshape(16, 128, LANES), "gx", 0, 0, axis_index_groups=chips, tiled=True
    )
    first = lift(0, band, f, top, left, right)
    pieces, first = lax.optimization_barrier((pieces, first))
    copies = mix(pieces, spec_re, spec_im)
    mixed = lax.all_to_all(copies, "gx", 0, 0, axis_index_groups=chips, tiled=True)
    last = lift(1, band, f, bottom, left, right)
    mixed, last = lax.optimization_barrier((mixed, last))
    mixed = mixed.reshape(2, ROWS, LANES)
    mixed_other = lax.ppermute(mixed, "gx", partner)
    first = first.reshape(2, 4, ROWS, LANES)
    last = last.reshape(2, 4, ROWS, LANES)
    result = finish(0, where, first, last, mixed, inverse, mlp_in, mlp_out)
    result = finish(2, where, first, last, mixed_other, inverse, mlp_in, mlp_out, result)
    return result.reshape(field.shape)


def solution(mesh):
    in_specs = (P("gy", None, None, "gx"), P(), P(), P(), P(), P())
    out_specs = P("gy", None, None, "gx")
    forward, inverse = tables(mesh.shape["gx"], LANES)
    return jax.shard_map(
        functools.partial(per_device, jnp.asarray(forward), jnp.asarray(inverse)),
        mesh=mesh, in_specs=in_specs, out_specs=out_specs, check_vma=False,
    )
```

```python
import functools
import math

import jax
import jax.numpy as jnp
import numpy as np
from jax import lax
from jax.experimental import pallas as pl
from jax.experimental.pallas import tpu as pltpu
from jax.sharding import PartitionSpec as P

BF = jnp.bfloat16
F32 = jnp.float32
LANES = 128
CH = 64
ROWS = 1024
PADDED = ROWS + 2 * CH
MODES = 16
HID = 256
CHUNK = 512
VMEM = pltpu.VMEM


def params(mib):
    return pltpu.CompilerParams(vmem_limit_bytes=mib * 2**20)


def cost(flops, read):
    return pl.CostEstimate(flops=int(flops), bytes_accessed=int(read), transcendentals=0)


def tables(blocks, width):
    total = blocks * width
    places = np.arange(-1, total + 1, dtype=np.int64)
    orders = np.arange(MODES, dtype=np.int64)
    phase = (places[:, None] * orders[None, :]) % total
    angle = phase.astype(np.float32) * np.float32(2.0 * math.pi / total)
    both = np.concatenate([np.cos(angle), -np.sin(angle)], axis=1).astype(np.float32)
    inside = both.copy()
    inside[0] = 0
    inside[-1] = 0
    forward = np.zeros((blocks, width, 3, 4, 2 * MODES), np.float32)
    inverse = np.zeros((blocks, 2 * MODES, width), np.float32)
    weight = np.where(orders == 0, 1.0, 2.0).astype(np.float32) / np.float32(total)
    weight = np.concatenate([weight, weight])
    for b in range(blocks):
        for d in range(3):
            first = b * width - d + 1 + 1
            forward[b, :, d, :, :] = inside[first : first + width][:, None, :]
        inverse[b] = (both[b * width + 1 : (b + 1) * width + 1] * weight).T
    forward = forward.reshape(blocks, width, 3 * 4 * 2 * MODES).astype(jnp.bfloat16)
    inverse = np.tile(inverse, (1, 4, 1))
    high = inverse.astype(jnp.bfloat16)
    low = (inverse - high.astype(np.float32)).astype(jnp.bfloat16)
    return forward, np.concatenate([high, low], axis=1)


def band_kernel(w_ref, o_ref):
    zero = jnp.zeros((CH, CH), BF)
    for a in range(3):
        for zo in range(2):
            for d in range(3):
                parts = []
                for zi in range(4):
                    b = zi - zo
                    parts.append(w_ref[(3 * a + b) * 3 + d] if 0 <= b <= 2 else zero)
                o_ref[a * 128 + zo * 64 : a * 128 + zo * 64 + 64, d * 256 : d * 256 + 256] = (
                    jnp.concatenate(parts, axis=1)
                )


def one_hot(height, pairs):
    x = lax.broadcasted_iota(jnp.int32, (height, LANES), 0)
    lane = lax.broadcasted_iota(jnp.int32, (height, LANES), 1)
    hit = jnp.zeros((height, LANES), F32)
    for row, column in pairs:
        hit = jnp.where((x == row) & (lane == column), 1.0, hit)
    return hit.astype(BF)


def group_mask(height, group):
    lane = lax.broadcasted_iota(jnp.int32, (height, LANES), 1)
    return lane // 32 == group


def dft_kernel(f_ref, t_ref, w_ref, g_ref, own_ref, e_ref, band_ref, tab_ref, f_buf, sem):
    fetch = [pltpu.make_async_copy(f_ref.at[y], f_buf.at[y], sem.at[y]) for y in range(16)]
    for i in range(4):
        for g in range(4):
            fetch[4 * g + i].start()
    band_kernel(w_ref, band_ref)
    for g in range(4):
        for d in range(3):
            part = t_ref[:, d * 128 : d * 128 + 128]
            tab_ref[g * 128 : g * 128 + 128, d * 128 : d * 128 + 128] = jnp.where(
                group_mask(128, g), part, jnp.zeros_like(part)
            )
    for i in range(4):
        for g in range(4):
            y = 4 * g + i
            tab_ref[g * 128 : g * 128 + 128, 384:512] = one_hot(
                128, [(127, 2 * y + 2), (0, 2 * y + 1)]
            )
        for g in range(4):
            fetch[4 * g + i].wait()

        @pl.loop(0, ROWS // CHUNK)
        def _(r):
            at = pl.ds(pl.multiple_of(r * CHUNK, CHUNK), CHUNK)
            left = jnp.concatenate([f_buf[4 * g + i, at, :] for g in range(4)], axis=1)
            out = jnp.dot(left, tab_ref[...], preferred_element_type=F32)
            for d in range(3):
                g_ref[i, d, at, :] = out[:, d * 128 : d * 128 + 128].astype(BF)
            own_ref[i, at, :] = out[:, 128:256]
            edge = out[:, 384:512].astype(BF)
            if i == 0:
                e_ref[at, :] = edge
            else:
                e_ref[at, :] = e_ref[at, :] + edge


def dft(field, table, conv_w):
    return pl.pallas_call(
        dft_kernel,
        in_specs=[pl.BlockSpec(memory_space=pltpu.HBM)] + [pl.BlockSpec(memory_space=VMEM)] * 2,
        out_shape=(
            jax.ShapeDtypeStruct((4, 3, ROWS, LANES), BF),
            jax.ShapeDtypeStruct((4, ROWS, LANES), F32),
            jax.ShapeDtypeStruct((ROWS, LANES), BF),
            jax.ShapeDtypeStruct((384, 768), BF),
        ),
        scratch_shapes=[
            VMEM((512, 512), BF),
            VMEM((16, ROWS, LANES), BF),
            pltpu.SemaphoreType.DMA((16,)),
        ],
        compiler_params=params(46),
        cost_estimate=cost(4e9, 4e6),
        name="dft",
    )(field, table, conv_w)


def halo_kernel(top_ref, bottom_ref, t_ref, e_in_ref, gt_ref, gb_ref, e_ref):
    def columns(pairs, group):
        parts = []
        for d in range(3):
            part = t_ref[:, d * 128 : d * 128 + 128]
            parts.append(jnp.where(group_mask(128, group), part, jnp.zeros_like(part)))
        return jnp.concatenate(parts + [one_hot(128, pairs)], axis=1)

    above = columns([(127, 0), (0, 127)], 0)
    below = columns([(127, 34), (0, 33)], 3)

    @pl.loop(0, ROWS // CHUNK)
    def _(r):
        at = pl.ds(pl.multiple_of(r * CHUNK, CHUNK), CHUNK)
        up = jnp.dot(top_ref[at, :], above, preferred_element_type=F32).astype(BF)
        down = jnp.dot(bottom_ref[at, :], below, preferred_element_type=F32).astype(BF)
        for d in range(3):
            gt_ref[d, at, :] = up[:, d * 128 : d * 128 + 128]
            gb_ref[d, at, :] = down[:, d * 128 : d * 128 + 128]
        e_ref[at, :] = e_in_ref[at, :] + up[:, 384:512] + down[:, 384:512]


def halo_modes(top, bottom, table, edges):
    return pl.pallas_call(
        halo_kernel,
        out_shape=(
            jax.ShapeDtypeStruct((3, ROWS, LANES), BF),
            jax.ShapeDtypeStruct((3, ROWS, LANES), BF),
            jax.ShapeDtypeStruct((ROWS, LANES), BF),
        ),
        compiler_params=params(32),
        cost_estimate=cost(1e9, 1e6),
        name="halo_modes",
    )(top, bottom, table, edges)


def clear(a1_ref, a2_ref):
    @pl.loop(0, 8)
    def _(g):
        at = pl.ds(pl.multiple_of(g * 128, 128), 128)
        a1_ref[at, :] = jnp.zeros((128, 256), F32)
        a2_ref[at, :] = jnp.zeros((128, 256), F32)


def clear_ends(planes):
    for plane in planes:
        plane[0:CH, :] = jnp.zeros((CH, LANES), BF)
        plane[CH + ROWS : PADDED, :] = jnp.zeros((CH, LANES), BF)


def band_step(p, half, w_ref, cells, a1_ref, a2_ref, s_ref, emit, after):
    for g in range(8):
        at = slice(g * 128, g * 128 + 128)
        part = jnp.dot(w_ref[...], cells(g * 128), preferred_element_type=F32)
        done = a2_ref[at, :] + part[256:384]
        a2_ref[at, :] = a1_ref[at, :] + part[128:256]
        a1_ref[at, :] = part[0:128]
        emit(jnp.maximum(p - 2, 0), at, done[:, 0:128])
        emit(p + half - 2, at, done[:, 128:256])
        s_ref[jnp.minimum(p, 2), at, :] = done[:, 128:256]
        after(g * 128)


def band_seam(half, a1_ref, a2_ref, s_ref, emit):
    for g in range(8):
        at = slice(g * 128, g * 128 + 128)
        emit(half - 2, at, a2_ref[at, 0:128] + s_ref[0, at, :])
        emit(half - 1, at, a1_ref[at, 0:128] + s_ref[1, at, :])


def conv_scratch():
    return [
        VMEM((ROWS, 256), F32),
        VMEM((ROWS, 256), F32),
        VMEM((3, ROWS, LANES), F32),
    ]


def spectral_kernel(
    at_ref, w_ref, g_ref, own_ref, gt_ref, gb_ref, e_ref, mine_ref, other_ref,
    x_ref, a1_ref, a2_ref, s_ref, o_ref
):
    clear(a1_ref, a2_ref)
    clear_ends([x_ref.at[r, d] for r in range(6) for d in range(3)])
    lane = lax.broadcasted_iota(jnp.int32, (256, LANES), 1)
    for r0 in range(0, ROWS, 256):
        src, dst = slice(r0, r0 + 256), slice(CH + r0, CH + r0 + 256)
        for d in range(3):
            for i in range(4):
                x_ref[i + 1, d, dst, :] = g_ref[i, d, src, :]
            x_ref[0, d, dst, :] = jnp.where(
                lane < 32, gt_ref[d, src, :], pltpu.roll(g_ref[3, d, src, :], 32, 1)
            )
            x_ref[5, d, dst, :] = jnp.where(
                lane >= 96, gb_ref[d, src, :], pltpu.roll(g_ref[0, d, src, :], 96, 1)
            )
    shift = 2 * at_ref[0]

    def emit(row, at, value):
        o_ref[(row + shift) % 4, at, :] = (value + own_ref[row, at, :]).astype(BF)

    @pl.loop(0, 3)
    def _(p):
        def cells(r0):
            rows = slice(r0, r0 + 256)
            return jnp.concatenate(
                [x_ref[layer, :, rows, :].reshape(768, LANES) for layer in (p, p + 3)], axis=1
            )

        band_step(p, 3, w_ref, cells, a1_ref, a2_ref, s_ref, emit, lambda r0: None)

    band_seam(3, a1_ref, a2_ref, s_ref, emit)
    mine_ref[...] = o_ref[0:2]
    other_ref[0:2] = o_ref[2:4]
    other_ref[2] = e_ref[...]


def spectral(where, band, modes, own, above, below, edges):
    return pl.pallas_call(
        spectral_kernel,
        in_specs=[pl.BlockSpec(memory_space=pltpu.SMEM)] + [pl.BlockSpec(memory_space=VMEM)] * 6,
        out_shape=(
            jax.ShapeDtypeStruct((2, ROWS, LANES), BF),
            jax.ShapeDtypeStruct((3, ROWS, LANES), BF),
        ),
        scratch_shapes=[VMEM((6, 3, PADDED, LANES), BF)]
        + conv_scratch()
        + [VMEM((4, ROWS, LANES), BF)],
        compiler_params=params(40),
        cost_estimate=cost(4e9, 8e6),
        name="spectral",
    )(where, band, modes, own, above, below, edges)


def add_kernel(a_ref, b_ref, o_ref):
    o_ref[...] = (a_ref[...].astype(F32) + b_ref[0:2].astype(F32)).astype(BF)


def add(a, b):
    return pl.pallas_call(
        add_kernel,
        out_shape=jax.ShapeDtypeStruct(a.shape, BF),
        compiler_params=params(16),
        cost_estimate=cost(1e6, 2e6),
        name="add",
    )(a, b)


def lift_kernel(
    part, at_ref, w_ref, f_ref, halo_ref, theirs_ref, across_ref, o_ref,
    w_buf, x_ref, even_ref, odd_ref, a1_ref, a2_ref, s_ref, ed_ref, o_buf, sem, in_sem, out_sem
):
    half = 5
    first = 8 * part
    body = slice(CH, CH + ROWS)
    edges = [
        pltpu.make_async_copy(theirs_ref.at[2], ed_ref.at[0], in_sem.at[0]),
        pltpu.make_async_copy(across_ref, ed_ref.at[1], in_sem.at[1]),
    ]
    weights = pltpu.make_async_copy(w_ref, w_buf, in_sem.at[2])
    fetch = []
    for r in range(10):
        src = halo_ref if first + r in (0, 17) else f_ref.at[first + r - 1]
        fetch.append(pltpu.make_async_copy(src, x_ref.at[r, body, :], sem.at[r]))
    later = [r + k for r in range(1, half) for k in (0, half) if r + k != half - 1]
    for copy in edges + [fetch[0], fetch[half], weights, fetch[half - 1]]:
        copy.start()
    for r in later:
        fetch[r].start()
    clear(a1_ref, a2_ref)
    clear_ends([x_ref.at[r] for r in range(2 * half)])
    clear_ends([ref.at[k, d] for ref in (even_ref, odd_ref) for k in range(2) for d in range(2)])
    lane = lax.broadcasted_iota(jnp.int32, (128, LANES), 1)
    for copy in edges:
        copy.wait()
    for r0 in range(0, ROWS, 128):
        at = slice(r0, r0 + 128)
        ed_ref[0, at, :] = jnp.where(
            (lane + at_ref[0]) % 2 == 1, ed_ref[0, at, :], ed_ref[1, at, :]
        )

    def build(into, p, r0):
        at = slice(CH + r0, CH + r0 + 128)
        for k in range(2):
            r = p + k * half
            mid = x_ref[r, at, :]
            edge = pltpu.roll(ed_ref[0, r0 : r0 + 128, :], 128 - 2 * (first + r), 1)
            into[k, 0, at, :] = jnp.where(lane == 0, edge, pltpu.roll(mid, 1, 1))
            into[k, 1, at, :] = jnp.where(lane == 127, edge, pltpu.roll(mid, 127, 1))

    fetch[0].wait()
    fetch[half].wait()
    for r0 in range(0, ROWS, 128):
        build(even_ref, 0, r0)
    weights.wait()
    fetch[half - 1].wait()

    def arrived(r):
        pltpu.make_async_copy(halo_ref, x_ref.at[r, body, :], sem.at[r]).wait()

    def out(row):
        return pltpu.make_async_copy(o_buf.at[row], o_ref.at[row], out_sem.at[row])

    def before(p):
        @pl.when(p < half - 2)
        def _():
            arrived(p + 1)

        @pl.when(p < half - 1)
        def _():
            arrived(p + 1 + half)

        @pl.when(p > 2)
        def _():
            out(p - 3).start()
            out(p + half - 3).start()

    def emit(row, at, value):
        same = x_ref[row + 1, CH + at.start : CH + at.stop, :].astype(F32)
        o_buf[row, at, :] = (value + same).astype(BF)

    def step(p, shifted, following):
        before(p)

        def cells(r0):
            rows = slice(r0, r0 + 256)
            sides = []
            for k in range(2):
                middle = x_ref[p + k * half, rows, :]
                sides.append(
                    jnp.concatenate(
                        [shifted[k, 0, rows, :], middle, shifted[k, 1, rows, :]], axis=0
                    )
                )
            return jnp.concatenate(sides, axis=1)

        def after(r0):
            if following is not None:
                build(following, p + 1, r0)

        band_step(p, half, w_buf, cells, a1_ref, a2_ref, s_ref, emit, after)

    @pl.loop(0, half // 2)
    def _(q):
        step(2 * q, even_ref, odd_ref)
        step(2 * q + 1, odd_ref, even_ref)

    step(jnp.int32(half - 1), even_ref, None)
    band_seam(half, a1_ref, a2_ref, s_ref, emit)
    for row in (half - 3, 2 * half - 3, half - 2, half - 1):
        out(row).start()
    for row in range(8):
        out(row).wait()


def lift(part, where, band, field, halo, theirs, across):
    anywhere = pl.BlockSpec(memory_space=pl.ANY)
    return pl.pallas_call(
        functools.partial(lift_kernel, part),
        in_specs=[pl.BlockSpec(memory_space=pltpu.SMEM)] + [anywhere] * 5,
        out_specs=anywhere,
        out_shape=jax.ShapeDtypeStruct((8, ROWS, LANES), BF),
        scratch_shapes=[
            VMEM((384, 768), BF),
            VMEM((10, PADDED, LANES), BF),
            VMEM((2, 2, PADDED, LANES), BF),
            VMEM((2, 2, PADDED, LANES), BF),
        ]
        + conv_scratch()
        + [
            VMEM((2, ROWS, LANES), BF),
            VMEM((8, ROWS, LANES), BF),
            pltpu.SemaphoreType.DMA((10,)),
            pltpu.SemaphoreType.DMA((3,)),
            pltpu.SemaphoreType.DMA((8,)),
        ],
        compiler_params=params(60),
        cost_estimate=cost(8e9, 8e6),
        name="lift",
    )(where, band, field, halo, theirs, across)


def split(x):
    high = x.astype(BF)
    return high, (x - high.astype(F32)).astype(BF)


def mix_kernel(p_ref, re_ref, im_ref, o_ref):
    total = p_ref[0].astype(F32)
    for i in range(1, 16):
        total = total + p_ref[i].astype(F32)
    both = jnp.concatenate([total[0:CH], total[CH : 2 * CH]], axis=1)
    lane = lax.broadcasted_iota(jnp.int32, (CH, 256), 1)
    is_re = lane % 32 < MODES
    turned = jnp.where(is_re, -pltpu.roll(both, 256 - MODES, 1), pltpu.roll(both, MODES, 1))
    bh, bl = split(both)
    th, tl = split(turned)
    dot = functools.partial(jnp.dot, preferred_element_type=F32)
    rh, rl = split(re_ref[...].reshape(MODES * CH, CH))
    ih, il = split(im_ref[...].reshape(MODES * CH, CH))
    high = jnp.concatenate([rh, ih], axis=1)
    low = jnp.concatenate([rl, il], axis=1)
    cells = jnp.concatenate([bh, th], axis=0)
    rest = jnp.concatenate([bl, tl], axis=0)
    every = dot(
        jnp.concatenate([high, low], axis=1), jnp.concatenate([cells, cells], axis=0)
    ) + dot(high, rest)
    mode = lane % MODES
    out = every[0:CH]
    for k in range(1, MODES):
        out = jnp.where(mode == k, every[k * CH : k * CH + CH], out)
    piece = jnp.concatenate([out[:, 0:128], out[:, 128:256]], axis=0).astype(BF)
    for i in range(16):
        o_ref[i] = piece


def mix(pieces, spec_re, spec_im):
    return pl.pallas_call(
        mix_kernel,
        out_shape=jax.ShapeDtypeStruct((16, 128, LANES), BF),
        compiler_params=params(16),
        cost_estimate=cost(5e8, 1e6),
        name="mix",
    )(pieces, spec_re, spec_im)


GELU_ONE = math.sqrt(2.0 / math.pi)
GELU_THREE = GELU_ONE * 0.044715


def finish_kernel(h_ref, la_ref, lb_ref, m_ref, inv_ref, up_ref, down_ref, *rest):
    o_ref, tab_ref = rest[-2:]

    @pl.when(pl.program_id(0) == 0)
    def _():
        row = lax.broadcasted_iota(jnp.int32, (256, LANES), 0)
        inv = inv_ref[0]
        for g in range(4):
            tab_ref[:, g * 128 : g * 128 + 128] = jnp.where(
                (row // 32) % 4 == g, inv, jnp.zeros_like(inv)
            )

    dot = functools.partial(jnp.dot, preferred_element_type=F32)
    m = m_ref[0]
    branch = dot(jnp.concatenate([m, m], axis=1), tab_ref[...])
    lifted = jnp.concatenate([ref[g, 0] for ref in (la_ref, lb_ref) for g in range(2)], axis=1)
    blended = (lifted.astype(F32) + branch).astype(BF)
    cells = jnp.concatenate(
        [blended[z * CH : z * CH + CH] for z in range(CHUNK // CH)], axis=1
    )
    half_down = (0.5 * down_ref[...].astype(F32)).astype(BF)
    x = dot(up_ref[...], cells)
    bend = jnp.tanh(x * (GELU_ONE + GELU_THREE * (x * x)))
    hidden = (x * bend + x).astype(BF)
    out = cells.astype(F32) + dot(half_down, hidden)
    for z in range(CHUNK // CH):
        for g in range(4):
            c = (z * 4 + g) * 128
            o_ref[g, 0, z * CH : z * CH + CH, :] = out[:, c : c + 128].astype(BF)


def finish(half_at, where, first, last, mixed, inverse, mlp_in, mlp_out, into=None):
    chunks = ROWS // CHUNK
    layer = lambda s, h: (0, 2 * h[half_at] + s // chunks, s % chunks, 0)
    fixed = lambda *shape: pl.BlockSpec(shape, lambda s, h: (0,) * len(shape))
    operands = [where, first, last, mixed, inverse, mlp_in, mlp_out]
    specs = [
        pl.BlockSpec((2, 1, CHUNK, LANES), layer),
        pl.BlockSpec((2, 1, CHUNK, LANES), layer),
        pl.BlockSpec((1, CHUNK, LANES), lambda s, h: (s // chunks, s % chunks, 0)),
        pl.BlockSpec((1, 256, LANES), lambda s, h: (h[1], 0, 0)),
        fixed(HID, CH),
        fixed(CH, HID),
    ]
    if into is not None:
        operands.append(into)
        specs.append(pl.BlockSpec(memory_space=pltpu.HBM))
    return pl.pallas_call(
        finish_kernel,
        grid_spec=pltpu.PrefetchScalarGridSpec(
            num_scalar_prefetch=1,
            grid=(2 * chunks,),
            in_specs=specs,
            out_specs=pl.BlockSpec((4, 1, CHUNK, LANES), layer),
            scratch_shapes=[VMEM((256, 512), BF)],
        ),
        out_shape=jax.ShapeDtypeStruct((4, 4, ROWS, LANES), BF),
        input_output_aliases={} if into is None else {7: 0},
        compiler_params=params(58),
        cost_estimate=cost(5e9, 6e6),
        name="finish",
    )(*operands)


def per_device(forward, inverse, field, conv_w, spec_re, spec_im, mlp_in, mlp_out):
    rows_y, depth, channels, width = field.shape
    blocks, layers = lax.axis_size("gx"), lax.axis_size("gy")
    place = lax.axis_index("gx")
    core = place % 2
    f = field.reshape(rows_y, depth * channels, width)

    up_y = [(i, i + 1) for i in range(layers - 1)]
    down_y = [(j, i) for i, j in up_y]
    neighbour = [(i, i + 1) for i in range(1, blocks - 1, 2)]
    neighbour = neighbour + [(j, i) for i, j in neighbour]
    partner = [(i, i ^ 1) for i in range(blocks)]
    chips = [[i for i in range(c, blocks, 2)] for c in range(2)]

    top = lax.ppermute(f[rows_y - 1], "gy", up_y)
    bottom = lax.ppermute(f[0], "gy", down_y)
    where = jnp.stack([core, place, 1 - core]).astype(jnp.int32)
    table = lax.dynamic_index_in_dim(forward, place, 0, keepdims=False)
    modes, own, edges, band = dft(f, table, conv_w)
    above, below, edges = halo_modes(top, bottom, table, edges)
    across = lax.ppermute(edges, "gx", neighbour)
    mine, other = spectral(where, band, modes, own, above, below, edges)
    other, across = lax.optimization_barrier((other, across))
    theirs = lax.ppermute(other, "gx", partner)
    chip_sum = add(mine, theirs)
    pieces = lax.all_to_all(
        chip_sum.reshape(16, 128, LANES), "gx", 0, 0, axis_index_groups=chips, tiled=True
    )
    first = lift(0, where, band, f, top, theirs, across)
    pieces, first = lax.optimization_barrier((pieces, first))
    copies = mix(pieces, spec_re, spec_im)
    mixed = lax.all_to_all(copies, "gx", 0, 0, axis_index_groups=chips, tiled=True)
    last = lift(1, where, band, f, bottom, theirs, across)
    mixed, last = lax.optimization_barrier((mixed, last))
    mixed = mixed.reshape(2, ROWS, LANES)
    mixed_other = lax.ppermute(mixed, "gx", partner)
    first = first.reshape(2, 4, ROWS, LANES)
    last = last.reshape(2, 4, ROWS, LANES)
    result = finish(0, where, first, last, mixed, inverse, mlp_in, mlp_out)
    result = finish(2, where, first, last, mixed_other, inverse, mlp_in, mlp_out, result)
    return result.reshape(field.shape)


def solution(mesh):
    in_specs = (P("gy", None, None, "gx"), P(), P(), P(), P(), P())
    out_specs = P("gy", None, None, "gx")
    forward, inverse = tables(mesh.shape["gx"], LANES)
    return jax.shard_map(
        functools.partial(per_device, jnp.asarray(forward), jnp.asarray(inverse)),
        mesh=mesh, in_specs=in_specs, out_specs=out_specs, check_vma=False,
    )
```

```python
import functools
import math

import jax
import jax.numpy as jnp
import numpy as np
from jax import lax
from jax.experimental import pallas as pl
from jax.experimental.pallas import tpu as pltpu
from jax.sharding import PartitionSpec as P

BF = jnp.bfloat16
F32 = jnp.float32
LANES = 128
CH = 64
ROWS = 1024
PADDED = ROWS + 2 * CH
MODES = 16
HID = 256
CHUNK = 512
VMEM = pltpu.VMEM


def params(mib):
    return pltpu.CompilerParams(vmem_limit_bytes=mib * 2**20)


def cost(flops, read):
    return pl.CostEstimate(flops=int(flops), bytes_accessed=int(read), transcendentals=0)


def tables(blocks, width):
    total = blocks * width
    places = np.arange(-1, total + 1, dtype=np.int64)
    orders = np.arange(MODES, dtype=np.int64)
    phase = (places[:, None] * orders[None, :]) % total
    angle = phase.astype(np.float32) * np.float32(2.0 * math.pi / total)
    both = np.concatenate([np.cos(angle), -np.sin(angle)], axis=1).astype(np.float32)
    inside = both.copy()
    inside[0] = 0
    inside[-1] = 0
    forward = np.zeros((blocks, width, 3, 4, 2 * MODES), np.float32)
    inverse = np.zeros((blocks, 2 * MODES, width), np.float32)
    weight = np.where(orders == 0, 1.0, 2.0).astype(np.float32) / np.float32(total)
    weight = np.concatenate([weight, weight])
    for b in range(blocks):
        for d in range(3):
            first = b * width - d + 1 + 1
            forward[b, :, d, :, :] = inside[first : first + width][:, None, :]
        inverse[b] = (both[b * width + 1 : (b + 1) * width + 1] * weight).T
    forward = forward.reshape(blocks, width, 3 * 4 * 2 * MODES).astype(jnp.bfloat16)
    inverse = np.tile(inverse, (1, 4, 1))
    high = inverse.astype(jnp.bfloat16)
    low = (inverse - high.astype(np.float32)).astype(jnp.bfloat16)
    return forward, np.concatenate([high, low], axis=1)


def band_kernel(w_ref, o_ref):
    zero = jnp.zeros((CH, CH), BF)
    for a in range(3):
        for zo in range(2):
            for d in range(3):
                parts = []
                for zi in range(4):
                    b = zi - zo
                    parts.append(w_ref[(3 * a + b) * 3 + d] if 0 <= b <= 2 else zero)
                o_ref[a * 128 + zo * 64 : a * 128 + zo * 64 + 64, d * 256 : d * 256 + 256] = (
                    jnp.concatenate(parts, axis=1)
                )


def one_hot(height, pairs):
    x = lax.broadcasted_iota(jnp.int32, (height, LANES), 0)
    lane = lax.broadcasted_iota(jnp.int32, (height, LANES), 1)
    hit = jnp.zeros((height, LANES), F32)
    for row, column in pairs:
        hit = jnp.where((x == row) & (lane == column), 1.0, hit)
    return hit.astype(BF)


def group_mask(height, group):
    lane = lax.broadcasted_iota(jnp.int32, (height, LANES), 1)
    return lane // 32 == group


def dft_kernel(
    f_ref, t_ref, w_ref, g_ref, own_ref, e_ref, band_ref, tab_ref, f_buf, w_buf, sem, w_sem
):
    weights = pltpu.make_async_copy(w_ref, w_buf, w_sem)
    weights.start()
    fetch = [pltpu.make_async_copy(f_ref.at[y], f_buf.at[y], sem.at[y]) for y in range(16)]
    for i in range(4):
        for g in range(4):
            fetch[4 * g + i].start()
    weights.wait()
    band_kernel(w_buf, band_ref)
    for g in range(4):
        for d in range(3):
            part = t_ref[:, d * 128 : d * 128 + 128]
            tab_ref[g * 128 : g * 128 + 128, d * 128 : d * 128 + 128] = jnp.where(
                group_mask(128, g), part, jnp.zeros_like(part)
            )
    for i in range(4):
        for g in range(4):
            y = 4 * g + i
            tab_ref[g * 128 : g * 128 + 128, 384:512] = one_hot(
                128, [(127, 2 * y + 2), (0, 2 * y + 1)]
            )
        for g in range(4):
            fetch[4 * g + i].wait()

        @pl.loop(0, ROWS // CHUNK)
        def _(r):
            at = pl.ds(pl.multiple_of(r * CHUNK, CHUNK), CHUNK)
            left = jnp.concatenate([f_buf[4 * g + i, at, :] for g in range(4)], axis=1)
            out = jnp.dot(left, tab_ref[...], preferred_element_type=F32)
            for d in range(3):
                g_ref[i, d, at, :] = out[:, d * 128 : d * 128 + 128].astype(BF)
            own_ref[i, at, :] = out[:, 128:256]
            edge = out[:, 384:512].astype(BF)
            if i == 0:
                e_ref[at, :] = edge
            else:
                e_ref[at, :] = e_ref[at, :] + edge


def dft(field, table, conv_w):
    return pl.pallas_call(
        dft_kernel,
        in_specs=[
            pl.BlockSpec(memory_space=pltpu.HBM),
            pl.BlockSpec(memory_space=VMEM),
            pl.BlockSpec(memory_space=pltpu.HBM),
        ],
        out_shape=(
            jax.ShapeDtypeStruct((4, 3, ROWS, LANES), BF),
            jax.ShapeDtypeStruct((4, ROWS, LANES), F32),
            jax.ShapeDtypeStruct((ROWS, LANES), BF),
            jax.ShapeDtypeStruct((384, 768), BF),
        ),
        scratch_shapes=[
            VMEM((512, 512), BF),
            VMEM((16, ROWS, LANES), BF),
            VMEM((27, CH, CH), BF),
            pltpu.SemaphoreType.DMA((16,)),
            pltpu.SemaphoreType.DMA,
        ],
        compiler_params=params(46),
        cost_estimate=cost(4e9, 4e6),
        name="dft",
    )(field, table, conv_w)


def halo_kernel(top_ref, bottom_ref, t_ref, e_in_ref, gt_ref, gb_ref, e_ref):
    def columns(pairs, group):
        parts = []
        for d in range(3):
            part = t_ref[:, d * 128 : d * 128 + 128]
            parts.append(jnp.where(group_mask(128, group), part, jnp.zeros_like(part)))
        return jnp.concatenate(parts + [one_hot(128, pairs)], axis=1)

    above = columns([(127, 0), (0, 127)], 0)
    below = columns([(127, 34), (0, 33)], 3)

    @pl.loop(0, ROWS // CHUNK)
    def _(r):
        at = pl.ds(pl.multiple_of(r * CHUNK, CHUNK), CHUNK)
        up = jnp.dot(top_ref[at, :], above, preferred_element_type=F32).astype(BF)
        down = jnp.dot(bottom_ref[at, :], below, preferred_element_type=F32).astype(BF)
        for d in range(3):
            gt_ref[d, at, :] = up[:, d * 128 : d * 128 + 128]
            gb_ref[d, at, :] = down[:, d * 128 : d * 128 + 128]
        e_ref[at, :] = e_in_ref[at, :] + up[:, 384:512] + down[:, 384:512]


def halo_modes(top, bottom, table, edges):
    return pl.pallas_call(
        halo_kernel,
        out_shape=(
            jax.ShapeDtypeStruct((3, ROWS, LANES), BF),
            jax.ShapeDtypeStruct((3, ROWS, LANES), BF),
            jax.ShapeDtypeStruct((ROWS, LANES), BF),
        ),
        compiler_params=params(32),
        cost_estimate=cost(1e9, 1e6),
        name="halo_modes",
    )(top, bottom, table, edges)


def clear(a1_ref, a2_ref):
    @pl.loop(0, 8)
    def _(g):
        at = pl.ds(pl.multiple_of(g * 128, 128), 128)
        a1_ref[at, :] = jnp.zeros((128, 256), F32)
        a2_ref[at, :] = jnp.zeros((128, 256), F32)


def clear_ends(planes):
    for plane in planes:
        plane[0:CH, :] = jnp.zeros((CH, LANES), BF)
        plane[CH + ROWS : PADDED, :] = jnp.zeros((CH, LANES), BF)


def band_step(p, half, w_ref, cells, a1_ref, a2_ref, s_ref, emit, after):
    for g in range(8):
        at = slice(g * 128, g * 128 + 128)
        part = jnp.dot(w_ref[...], cells(g * 128), preferred_element_type=F32)
        done = a2_ref[at, :] + part[256:384]
        a2_ref[at, :] = a1_ref[at, :] + part[128:256]
        a1_ref[at, :] = part[0:128]
        emit(jnp.maximum(p - 2, 0), at, done[:, 0:128])
        emit(p + half - 2, at, done[:, 128:256])
        s_ref[jnp.minimum(p, 2), at, :] = done[:, 128:256]
        after(g * 128)


def band_seam(half, a1_ref, a2_ref, s_ref, emit):
    for g in range(8):
        at = slice(g * 128, g * 128 + 128)
        emit(half - 2, at, a2_ref[at, 0:128] + s_ref[0, at, :])
        emit(half - 1, at, a1_ref[at, 0:128] + s_ref[1, at, :])


def conv_scratch():
    return [
        VMEM((ROWS, 256), F32),
        VMEM((ROWS, 256), F32),
        VMEM((3, ROWS, LANES), F32),
    ]


def spectral_kernel(
    at_ref, w_ref, g_ref, own_ref, gt_ref, gb_ref, e_ref, mine_ref, other_ref,
    x_ref, a1_ref, a2_ref, s_ref, o_ref
):
    clear(a1_ref, a2_ref)
    clear_ends([x_ref.at[r, d] for r in range(6) for d in range(3)])
    lane = lax.broadcasted_iota(jnp.int32, (256, LANES), 1)
    for r0 in range(0, ROWS, 256):
        src, dst = slice(r0, r0 + 256), slice(CH + r0, CH + r0 + 256)
        for d in range(3):
            for i in range(4):
                x_ref[i + 1, d, dst, :] = g_ref[i, d, src, :]
            x_ref[0, d, dst, :] = jnp.where(
                lane < 32, gt_ref[d, src, :], pltpu.roll(g_ref[3, d, src, :], 32, 1)
            )
            x_ref[5, d, dst, :] = jnp.where(
                lane >= 96, gb_ref[d, src, :], pltpu.roll(g_ref[0, d, src, :], 96, 1)
            )
    shift = 2 * at_ref[0]

    def emit(row, at, value):
        o_ref[(row + shift) % 4, at, :] = (value + own_ref[row, at, :]).astype(BF)

    @pl.loop(0, 3)
    def _(p):
        def cells(r0):
            rows = slice(r0, r0 + 256)
            return jnp.concatenate(
                [x_ref[layer, :, rows, :].reshape(768, LANES) for layer in (p, p + 3)], axis=1
            )

        band_step(p, 3, w_ref, cells, a1_ref, a2_ref, s_ref, emit, lambda r0: None)

    band_seam(3, a1_ref, a2_ref, s_ref, emit)
    mine_ref[...] = o_ref[0:2]
    other_ref[0:2] = o_ref[2:4]
    other_ref[2] = e_ref[...]


def spectral(where, band, modes, own, above, below, edges):
    return pl.pallas_call(
        spectral_kernel,
        in_specs=[pl.BlockSpec(memory_space=pltpu.SMEM)] + [pl.BlockSpec(memory_space=VMEM)] * 6,
        out_shape=(
            jax.ShapeDtypeStruct((2, ROWS, LANES), BF),
            jax.ShapeDtypeStruct((3, ROWS, LANES), BF),
        ),
        scratch_shapes=[VMEM((6, 3, PADDED, LANES), BF)]
        + conv_scratch()
        + [VMEM((4, ROWS, LANES), BF)],
        compiler_params=params(40),
        cost_estimate=cost(4e9, 8e6),
        name="spectral",
    )(where, band, modes, own, above, below, edges)


def add_kernel(a_ref, b_ref, o_ref):
    o_ref[...] = (a_ref[...].astype(F32) + b_ref[0:2].astype(F32)).astype(BF)


def add(a, b):
    return pl.pallas_call(
        add_kernel,
        out_shape=jax.ShapeDtypeStruct(a.shape, BF),
        compiler_params=params(16),
        cost_estimate=cost(1e6, 2e6),
        name="add",
    )(a, b)


def lift_kernel(
    part, at_ref, w_ref, f_ref, halo_ref, theirs_ref, across_ref, o_ref,
    w_buf, x_ref, even_ref, odd_ref, a1_ref, a2_ref, s_ref, ed_ref, o_buf, sem, in_sem, out_sem
):
    half = 5
    first = 8 * part
    body = slice(CH, CH + ROWS)
    edges = [
        pltpu.make_async_copy(theirs_ref.at[2], ed_ref.at[0], in_sem.at[0]),
        pltpu.make_async_copy(across_ref, ed_ref.at[1], in_sem.at[1]),
    ]
    weights = pltpu.make_async_copy(w_ref, w_buf, in_sem.at[2])
    fetch = []
    for r in range(10):
        src = halo_ref if first + r in (0, 17) else f_ref.at[first + r - 1]
        fetch.append(pltpu.make_async_copy(src, x_ref.at[r, body, :], sem.at[r]))
    later = [r + k for r in range(1, half) for k in (0, half) if r + k != half - 1]
    for copy in edges + [fetch[0], fetch[half], weights, fetch[half - 1]]:
        copy.start()
    for r in later:
        fetch[r].start()
    clear(a1_ref, a2_ref)
    clear_ends([x_ref.at[r] for r in range(2 * half)])
    clear_ends([ref.at[k, d] for ref in (even_ref, odd_ref) for k in range(2) for d in range(2)])
    lane = lax.broadcasted_iota(jnp.int32, (128, LANES), 1)
    for copy in edges:
        copy.wait()
    for r0 in range(0, ROWS, 128):
        at = slice(r0, r0 + 128)
        ed_ref[0, at, :] = jnp.where(
            (lane + at_ref[0]) % 2 == 1, ed_ref[0, at, :], ed_ref[1, at, :]
        )

    def build(into, p, r0):
        at = slice(CH + r0, CH + r0 + 128)
        for k in range(2):
            r = p + k * half
            mid = x_ref[r, at, :]
            edge = pltpu.roll(ed_ref[0, r0 : r0 + 128, :], 128 - 2 * (first + r), 1)
            into[k, 0, at, :] = jnp.where(lane == 0, edge, pltpu.roll(mid, 1, 1))
            into[k, 1, at, :] = jnp.where(lane == 127, edge, pltpu.roll(mid, 127, 1))

    fetch[0].wait()
    fetch[half].wait()
    for r0 in range(0, ROWS, 128):
        build(even_ref, 0, r0)
    weights.wait()
    fetch[half - 1].wait()

    def arrived(r):
        pltpu.make_async_copy(halo_ref, x_ref.at[r, body, :], sem.at[r]).wait()

    def out(row):
        return pltpu.make_async_copy(o_buf.at[row], o_ref.at[row], out_sem.at[row])

    def before(p):
        @pl.when(p < half - 2)
        def _():
            arrived(p + 1)

        @pl.when(p < half - 1)
        def _():
            arrived(p + 1 + half)

        @pl.when(p > 2)
        def _():
            out(p - 3).start()
            out(p + half - 3).start()

    def emit(row, at, value):
        same = x_ref[row + 1, CH + at.start : CH + at.stop, :].astype(F32)
        o_buf[row, at, :] = (value + same).astype(BF)

    def step(p, shifted, following):
        before(p)

        def cells(r0):
            rows = slice(r0, r0 + 256)
            sides = []
            for k in range(2):
                middle = x_ref[p + k * half, rows, :]
                sides.append(
                    jnp.concatenate(
                        [shifted[k, 0, rows, :], middle, shifted[k, 1, rows, :]], axis=0
                    )
                )
            return jnp.concatenate(sides, axis=1)

        def after(r0):
            if following is not None:
                build(following, p + 1, r0)

        band_step(p, half, w_buf, cells, a1_ref, a2_ref, s_ref, emit, after)

    @pl.loop(0, half // 2)
    def _(q):
        step(2 * q, even_ref, odd_ref)
        step(2 * q + 1, odd_ref, even_ref)

    step(jnp.int32(half - 1), even_ref, None)
    band_seam(half, a1_ref, a2_ref, s_ref, emit)
    for row in (half - 3, 2 * half - 3, half - 2, half - 1):
        out(row).start()
    for row in range(8):
        out(row).wait()


def lift(part, where, band, field, halo, theirs, across):
    anywhere = pl.BlockSpec(memory_space=pl.ANY)
    return pl.pallas_call(
        functools.partial(lift_kernel, part),
        in_specs=[pl.BlockSpec(memory_space=pltpu.SMEM)] + [anywhere] * 5,
        out_specs=anywhere,
        out_shape=jax.ShapeDtypeStruct((8, ROWS, LANES), BF),
        scratch_shapes=[
            VMEM((384, 768), BF),
            VMEM((10, PADDED, LANES), BF),
            VMEM((2, 2, PADDED, LANES), BF),
            VMEM((2, 2, PADDED, LANES), BF),
        ]
        + conv_scratch()
        + [
            VMEM((2, ROWS, LANES), BF),
            VMEM((8, ROWS, LANES), BF),
            pltpu.SemaphoreType.DMA((10,)),
            pltpu.SemaphoreType.DMA((3,)),
            pltpu.SemaphoreType.DMA((8,)),
        ],
        compiler_params=params(60),
        cost_estimate=cost(8e9, 8e6),
        name="lift",
    )(where, band, field, halo, theirs, across)


def split(x):
    high = x.astype(BF)
    return high, (x - high.astype(F32)).astype(BF)


def mix_kernel(p_ref, re_ref, im_ref, o_ref):
    total = p_ref[0].astype(F32)
    for i in range(1, 16):
        total = total + p_ref[i].astype(F32)
    both = jnp.concatenate([total[0:CH], total[CH : 2 * CH]], axis=1)
    lane = lax.broadcasted_iota(jnp.int32, (CH, 256), 1)
    is_re = lane % 32 < MODES
    turned = jnp.where(is_re, -pltpu.roll(both, 256 - MODES, 1), pltpu.roll(both, MODES, 1))
    bh, bl = split(both)
    th, tl = split(turned)
    dot = functools.partial(jnp.dot, preferred_element_type=F32)
    rh, rl = split(re_ref[...].reshape(MODES * CH, CH))
    ih, il = split(im_ref[...].reshape(MODES * CH, CH))
    high = jnp.concatenate([rh, ih], axis=1)
    low = jnp.concatenate([rl, il], axis=1)
    cells = jnp.concatenate([bh, th], axis=0)
    rest = jnp.concatenate([bl, tl], axis=0)
    every = dot(
        jnp.concatenate([high, low], axis=1), jnp.concatenate([cells, cells], axis=0)
    ) + dot(high, rest)
    mode = lane % MODES
    out = every[0:CH]
    for k in range(1, MODES):
        out = jnp.where(mode == k, every[k * CH : k * CH + CH], out)
    piece = jnp.concatenate([out[:, 0:128], out[:, 128:256]], axis=0).astype(BF)
    for i in range(16):
        o_ref[i] = piece


def mix(pieces, spec_re, spec_im):
    return pl.pallas_call(
        mix_kernel,
        out_shape=jax.ShapeDtypeStruct((16, 128, LANES), BF),
        compiler_params=params(16),
        cost_estimate=cost(5e8, 1e6),
        name="mix",
    )(pieces, spec_re, spec_im)


GELU_ONE = math.sqrt(2.0 / math.pi)
GELU_THREE = GELU_ONE * 0.044715


def finish_kernel(h_ref, la_ref, lb_ref, m_ref, inv_ref, up_ref, down_ref, *rest):
    o_ref, tab_ref, up_buf = rest[-3:]

    @pl.when(pl.program_id(0) == 0)
    def _():
        up_buf[...] = jnp.transpose(up_ref[...].astype(F32)).astype(BF)
        row = lax.broadcasted_iota(jnp.int32, (256, LANES), 0)
        inv = inv_ref[0]
        for g in range(4):
            tab_ref[:, g * 128 : g * 128 + 128] = jnp.where(
                (row // 32) % 4 == g, inv, jnp.zeros_like(inv)
            )

    dot = functools.partial(jnp.dot, preferred_element_type=F32)
    m = m_ref[0]
    branch = dot(jnp.concatenate([m, m], axis=1), tab_ref[...])
    lifted = jnp.concatenate([ref[g, 0] for ref in (la_ref, lb_ref) for g in range(2)], axis=1)
    blended = (lifted.astype(F32) + branch).astype(BF)
    cells = jnp.concatenate(
        [blended[z * CH : z * CH + CH] for z in range(CHUNK // CH)], axis=1
    )
    half_down = (0.5 * down_ref[...].astype(F32)).astype(BF)
    x = dot(up_buf[...], cells)
    bend = jnp.tanh(x * (GELU_ONE + GELU_THREE * (x * x)))
    hidden = (x * bend + x).astype(BF)
    out = cells.astype(F32) + dot(half_down, hidden)
    for z in range(CHUNK // CH):
        for g in range(4):
            c = (z * 4 + g) * 128
            o_ref[g, 0, z * CH : z * CH + CH, :] = out[:, c : c + 128].astype(BF)


def finish(half_at, where, first, last, mixed, inverse, mlp_in, mlp_out, into=None):
    chunks = ROWS // CHUNK
    layer = lambda s, h: (0, 2 * h[half_at] + s // chunks, s % chunks, 0)
    fixed = lambda *shape: pl.BlockSpec(shape, lambda s, h: (0,) * len(shape))
    operands = [where, first, last, mixed, inverse, mlp_in.T, mlp_out]
    specs = [
        pl.BlockSpec((2, 1, CHUNK, LANES), layer),
        pl.BlockSpec((2, 1, CHUNK, LANES), layer),
        pl.BlockSpec((1, CHUNK, LANES), lambda s, h: (s // chunks, s % chunks, 0)),
        pl.BlockSpec((1, 256, LANES), lambda s, h: (h[1], 0, 0)),
        fixed(CH, HID),
        fixed(CH, HID),
    ]
    if into is not None:
        operands.append(into)
        specs.append(pl.BlockSpec(memory_space=pltpu.HBM))
    return pl.pallas_call(
        finish_kernel,
        grid_spec=pltpu.PrefetchScalarGridSpec(
            num_scalar_prefetch=1,
            grid=(2 * chunks,),
            in_specs=specs,
            out_specs=pl.BlockSpec((4, 1, CHUNK, LANES), layer),
            scratch_shapes=[VMEM((256, 512), BF), VMEM((HID, CH), BF)],
        ),
        out_shape=jax.ShapeDtypeStruct((4, 4, ROWS, LANES), BF),
        input_output_aliases={} if into is None else {7: 0},
        compiler_params=params(52),
        cost_estimate=cost(5e9, 6e6),
        name="finish",
    )(*operands)


def per_device(forward, inverse, field, conv_w, spec_re, spec_im, mlp_in, mlp_out):
    rows_y, depth, channels, width = field.shape
    blocks, layers = lax.axis_size("gx"), lax.axis_size("gy")
    place = lax.axis_index("gx")
    core = place % 2
    f = field.reshape(rows_y, depth * channels, width)

    up_y = [(i, i + 1) for i in range(layers - 1)]
    down_y = [(j, i) for i, j in up_y]
    neighbour = [(i, i + 1) for i in range(1, blocks - 1, 2)]
    neighbour = neighbour + [(j, i) for i, j in neighbour]
    partner = [(i, i ^ 1) for i in range(blocks)]
    chips = [[i for i in range(c, blocks, 2)] for c in range(2)]

    top = lax.ppermute(f[rows_y - 1], "gy", up_y)
    bottom = lax.ppermute(f[0], "gy", down_y)
    where = jnp.stack([core, place, 1 - core]).astype(jnp.int32)
    table = lax.dynamic_index_in_dim(forward, place, 0, keepdims=False)
    modes, own, edges, band = dft(f, table, conv_w)
    above, below, edges = halo_modes(top, bottom, table, edges)
    across = lax.ppermute(edges, "gx", neighbour)
    mine, other = spectral(where, band, modes, own, above, below, edges)
    other, across = lax.optimization_barrier((other, across))
    theirs = lax.ppermute(other, "gx", partner)
    chip_sum = add(mine, theirs)
    pieces = lax.all_to_all(
        chip_sum.reshape(16, 128, LANES), "gx", 0, 0, axis_index_groups=chips, tiled=True
    )
    first = lift(0, where, band, f, top, theirs, across)
    pieces, first = lax.optimization_barrier((pieces, first))
    copies = mix(pieces, spec_re, spec_im)
    mixed = lax.all_to_all(copies, "gx", 0, 0, axis_index_groups=chips, tiled=True)
    last = lift(1, where, band, f, bottom, theirs, across)
    mixed, last = lax.optimization_barrier((mixed, last))
    mixed = mixed.reshape(2, ROWS, LANES)
    mixed_other = lax.ppermute(mixed, "gx", partner)
    first = first.reshape(2, 4, ROWS, LANES)
    last = last.reshape(2, 4, ROWS, LANES)
    result = finish(0, where, first, last, mixed, inverse, mlp_in, mlp_out)
    result = finish(2, where, first, last, mixed_other, inverse, mlp_in, mlp_out, result)
    return result.reshape(field.shape)


def solution(mesh):
    in_specs = (P("gy", None, None, "gx"), P(), P(), P(), P(), P())
    out_specs = P("gy", None, None, "gx")
    forward, inverse = tables(mesh.shape["gx"], LANES)
    return jax.shard_map(
        functools.partial(per_device, jnp.asarray(forward), jnp.asarray(inverse)),
        mesh=mesh, in_specs=in_specs, out_specs=out_specs, check_vma=False,
    )
```

```python
import functools
import math

import jax
import jax.numpy as jnp
import numpy as np
from jax import lax
from jax.experimental import pallas as pl
from jax.experimental.pallas import tpu as pltpu
from jax.sharding import PartitionSpec as P

BF = jnp.bfloat16
F32 = jnp.float32
LANES = 128
CH = 64
ROWS = 1024
PADDED = ROWS + 2 * CH
MODES = 16
HID = 256
CHUNK = 512
VMEM = pltpu.VMEM


def params(mib):
    return pltpu.CompilerParams(vmem_limit_bytes=mib * 2**20)


def cost(flops, read):
    return pl.CostEstimate(flops=int(flops), bytes_accessed=int(read), transcendentals=0)


def tables(blocks, width):
    total = blocks * width
    places = np.arange(-1, total + 1, dtype=np.int64)
    orders = np.arange(MODES, dtype=np.int64)
    phase = (places[:, None] * orders[None, :]) % total
    angle = phase.astype(np.float32) * np.float32(2.0 * math.pi / total)
    both = np.concatenate([np.cos(angle), -np.sin(angle)], axis=1).astype(np.float32)
    inside = both.copy()
    inside[0] = 0
    inside[-1] = 0
    forward = np.zeros((blocks, width, 3, 4, 2 * MODES), np.float32)
    inverse = np.zeros((blocks, 2 * MODES, width), np.float32)
    weight = np.where(orders == 0, 1.0, 2.0).astype(np.float32) / np.float32(total)
    weight = np.concatenate([weight, weight])
    for b in range(blocks):
        for d in range(3):
            first = b * width - d + 1 + 1
            forward[b, :, d, :, :] = inside[first : first + width][:, None, :]
        inverse[b] = (both[b * width + 1 : (b + 1) * width + 1] * weight).T
    forward = forward.reshape(blocks, width, 3 * 4 * 2 * MODES).astype(jnp.bfloat16)
    inverse = np.tile(inverse, (1, 4, 1))
    high = inverse.astype(jnp.bfloat16)
    low = (inverse - high.astype(np.float32)).astype(jnp.bfloat16)
    return forward, np.concatenate([high, low], axis=1)


def band_kernel(w_ref, o_ref):
    zero = jnp.zeros((CH, CH), BF)
    for a in range(3):
        for zo in range(2):
            for d in range(3):
                parts = []
                for zi in range(4):
                    b = zi - zo
                    parts.append(w_ref[(3 * a + b) * 3 + d] if 0 <= b <= 2 else zero)
                o_ref[a * 128 + zo * 64 : a * 128 + zo * 64 + 64, d * 256 : d * 256 + 256] = (
                    jnp.concatenate(parts, axis=1)
                )


def one_hot(height, pairs):
    x = lax.broadcasted_iota(jnp.int32, (height, LANES), 0)
    lane = lax.broadcasted_iota(jnp.int32, (height, LANES), 1)
    hit = jnp.zeros((height, LANES), F32)
    for row, column in pairs:
        hit = jnp.where((x == row) & (lane == column), 1.0, hit)
    return hit.astype(BF)


def group_mask(height, group):
    lane = lax.broadcasted_iota(jnp.int32, (height, LANES), 1)
    return lane // 32 == group


def dft_kernel(
    f_ref, t_ref, w_ref, g_ref, own_ref, e_ref, band_ref, tab_ref, f_buf, w_buf, sem, w_sem
):
    weights = pltpu.make_async_copy(w_ref, w_buf, w_sem)
    weights.start()
    fetch = [pltpu.make_async_copy(f_ref.at[y], f_buf.at[y], sem.at[y]) for y in range(16)]
    for i in range(4):
        for g in range(4):
            fetch[4 * g + i].start()
    weights.wait()
    band_kernel(w_buf, band_ref)
    for g in range(4):
        for d in range(3):
            part = t_ref[:, d * 128 : d * 128 + 128]
            tab_ref[g * 128 : g * 128 + 128, d * 128 : d * 128 + 128] = jnp.where(
                group_mask(128, g), part, jnp.zeros_like(part)
            )
    for i in range(4):
        for g in range(4):
            y = 4 * g + i
            tab_ref[g * 128 : g * 128 + 128, 384:512] = one_hot(
                128, [(127, 2 * y + 2), (0, 2 * y + 1)]
            )
        for g in range(4):
            fetch[4 * g + i].wait()

        @pl.loop(0, ROWS // CHUNK)
        def _(r):
            at = pl.ds(pl.multiple_of(r * CHUNK, CHUNK), CHUNK)
            left = jnp.concatenate([f_buf[4 * g + i, at, :] for g in range(4)], axis=1)
            out = jnp.dot(left, tab_ref[...], preferred_element_type=F32)
            for d in range(3):
                g_ref[i, d, at, :] = out[:, d * 128 : d * 128 + 128].astype(BF)
            own_ref[i, at, :] = out[:, 128:256]
            edge = out[:, 384:512].astype(BF)
            if i == 0:
                e_ref[at, :] = edge
            else:
                e_ref[at, :] = e_ref[at, :] + edge


def dft(field, table, conv_w):
    return pl.pallas_call(
        dft_kernel,
        in_specs=[
            pl.BlockSpec(memory_space=pltpu.HBM),
            pl.BlockSpec(memory_space=VMEM),
            pl.BlockSpec(memory_space=pltpu.HBM),
        ],
        out_shape=(
            jax.ShapeDtypeStruct((4, 3, ROWS, LANES), BF),
            jax.ShapeDtypeStruct((4, ROWS, LANES), F32),
            jax.ShapeDtypeStruct((ROWS, LANES), BF),
            jax.ShapeDtypeStruct((384, 768), BF),
        ),
        scratch_shapes=[
            VMEM((512, 512), BF),
            VMEM((16, ROWS, LANES), BF),
            VMEM((27, CH, CH), BF),
            pltpu.SemaphoreType.DMA((16,)),
            pltpu.SemaphoreType.DMA,
        ],
        compiler_params=params(46),
        cost_estimate=cost(4e9, 4e6),
        name="dft",
    )(field, table, conv_w)


def halo_kernel(top_ref, bottom_ref, t_ref, e_in_ref, gt_ref, gb_ref, e_ref):
    def columns(pairs, group):
        parts = []
        for d in range(3):
            part = t_ref[:, d * 128 : d * 128 + 128]
            parts.append(jnp.where(group_mask(128, group), part, jnp.zeros_like(part)))
        return jnp.concatenate(parts + [one_hot(128, pairs)], axis=1)

    above = columns([(127, 0), (0, 127)], 0)
    below = columns([(127, 34), (0, 33)], 3)

    @pl.loop(0, ROWS // CHUNK)
    def _(r):
        at = pl.ds(pl.multiple_of(r * CHUNK, CHUNK), CHUNK)
        up = jnp.dot(top_ref[at, :], above, preferred_element_type=F32).astype(BF)
        down = jnp.dot(bottom_ref[at, :], below, preferred_element_type=F32).astype(BF)
        for d in range(3):
            gt_ref[d, at, :] = up[:, d * 128 : d * 128 + 128]
            gb_ref[d, at, :] = down[:, d * 128 : d * 128 + 128]
        e_ref[at, :] = e_in_ref[at, :] + up[:, 384:512] + down[:, 384:512]


def halo_modes(top, bottom, table, edges):
    return pl.pallas_call(
        halo_kernel,
        out_shape=(
            jax.ShapeDtypeStruct((3, ROWS, LANES), BF),
            jax.ShapeDtypeStruct((3, ROWS, LANES), BF),
            jax.ShapeDtypeStruct((ROWS, LANES), BF),
        ),
        compiler_params=params(32),
        cost_estimate=cost(1e9, 1e6),
        name="halo_modes",
    )(top, bottom, table, edges)


def clear_ends(planes):
    for plane in planes:
        plane[0:CH, :] = jnp.zeros((CH, LANES), BF)
        plane[CH + ROWS : PADDED, :] = jnp.zeros((CH, LANES), BF)


def band_step(p, half, w_ref, cells, a1_ref, a2_ref, s_ref, emit, after):
    for g in range(8):
        at = slice(g * 128, g * 128 + 128)
        part = jnp.dot(w_ref[...], cells(g * 128), preferred_element_type=F32)
        done = part[256:384] + a2_ref[at, :] if p > 0 else part[256:384]
        a2_ref[at, :] = part[128:256] + a1_ref[at, :] if p > 0 else part[128:256]
        a1_ref[at, :] = part[0:128]
        if p >= 2:
            emit(p - 2, at, done[:, 0:128])
            emit(p + half - 2, at, done[:, 128:256])
        else:
            s_ref[p, at, :] = done[:, 128:256]
        after(g * 128)


def band_seam(half, a1_ref, a2_ref, s_ref, emit):
    for g in range(8):
        at = slice(g * 128, g * 128 + 128)
        emit(half - 2, at, a2_ref[at, 0:128] + s_ref[0, at, :])
        emit(half - 1, at, a1_ref[at, 0:128] + s_ref[1, at, :])


def conv_scratch():
    return [
        VMEM((ROWS, 256), F32),
        VMEM((ROWS, 256), F32),
        VMEM((2, ROWS, LANES), F32),
    ]


def spectral_kernel(
    at_ref, w_ref, g_ref, own_ref, gt_ref, gb_ref, e_ref, mine_ref, other_ref,
    x_ref, a1_ref, a2_ref, s_ref, o_ref
):
    clear_ends([x_ref.at[r, d] for r in range(6) for d in range(3)])
    lane = lax.broadcasted_iota(jnp.int32, (256, LANES), 1)
    for r0 in range(0, ROWS, 256):
        src, dst = slice(r0, r0 + 256), slice(CH + r0, CH + r0 + 256)
        for d in range(3):
            for i in range(4):
                x_ref[i + 1, d, dst, :] = g_ref[i, d, src, :]
            x_ref[0, d, dst, :] = jnp.where(
                lane < 32, gt_ref[d, src, :], pltpu.roll(g_ref[3, d, src, :], 32, 1)
            )
            x_ref[5, d, dst, :] = jnp.where(
                lane >= 96, gb_ref[d, src, :], pltpu.roll(g_ref[0, d, src, :], 96, 1)
            )
    shift = 2 * at_ref[0]

    def emit(row, at, value):
        o_ref[(row + shift) % 4, at, :] = (value + own_ref[row, at, :]).astype(BF)

    for p in range(3):

        def cells(r0, p=p):
            rows = slice(r0, r0 + 256)
            return jnp.concatenate(
                [x_ref[layer, :, rows, :].reshape(768, LANES) for layer in (p, p + 3)], axis=1
            )

        band_step(p, 3, w_ref, cells, a1_ref, a2_ref, s_ref, emit, lambda r0: None)

    band_seam(3, a1_ref, a2_ref, s_ref, emit)
    mine_ref[...] = o_ref[0:2]
    other_ref[0:2] = o_ref[2:4]
    other_ref[2] = e_ref[...]


def spectral(where, band, modes, own, above, below, edges):
    return pl.pallas_call(
        spectral_kernel,
        in_specs=[pl.BlockSpec(memory_space=pltpu.SMEM)] + [pl.BlockSpec(memory_space=VMEM)] * 6,
        out_shape=(
            jax.ShapeDtypeStruct((2, ROWS, LANES), BF),
            jax.ShapeDtypeStruct((3, ROWS, LANES), BF),
        ),
        scratch_shapes=[VMEM((6, 3, PADDED, LANES), BF)]
        + conv_scratch()
        + [VMEM((4, ROWS, LANES), BF)],
        compiler_params=params(40),
        cost_estimate=cost(4e9, 8e6),
        name="spectral",
    )(where, band, modes, own, above, below, edges)


def add_kernel(a_ref, b_ref, o_ref):
    o_ref[...] = (a_ref[...].astype(F32) + b_ref[0:2].astype(F32)).astype(BF)


def add(a, b):
    return pl.pallas_call(
        add_kernel,
        out_shape=jax.ShapeDtypeStruct(a.shape, BF),
        compiler_params=params(16),
        cost_estimate=cost(1e6, 2e6),
        name="add",
    )(a, b)


def lift_kernel(
    part, at_ref, w_ref, f_ref, halo_ref, theirs_ref, across_ref, o_ref,
    w_buf, x_ref, even_ref, odd_ref, a1_ref, a2_ref, s_ref, ed_ref, o_buf, sem, in_sem, out_sem
):
    half = 5
    first = 8 * part
    body = slice(CH, CH + ROWS)
    edges = [
        pltpu.make_async_copy(theirs_ref.at[2], ed_ref.at[0], in_sem.at[0]),
        pltpu.make_async_copy(across_ref, ed_ref.at[1], in_sem.at[1]),
    ]
    weights = pltpu.make_async_copy(w_ref, w_buf, in_sem.at[2])
    fetch = []
    for r in range(10):
        src = halo_ref if first + r in (0, 17) else f_ref.at[first + r - 1]
        fetch.append(pltpu.make_async_copy(src, x_ref.at[r, body, :], sem.at[r]))
    later = [r + k for r in range(1, half) for k in (0, half) if r + k != half - 1]
    for copy in edges + [fetch[0], fetch[half], weights, fetch[half - 1]]:
        copy.start()
    for r in later:
        fetch[r].start()
    clear_ends([x_ref.at[r] for r in range(2 * half)])
    clear_ends([ref.at[k, d] for ref in (even_ref, odd_ref) for k in range(2) for d in range(2)])
    lane = lax.broadcasted_iota(jnp.int32, (128, LANES), 1)
    for copy in edges:
        copy.wait()
    for r0 in range(0, ROWS, 128):
        at = slice(r0, r0 + 128)
        ed_ref[0, at, :] = jnp.where(
            (lane + at_ref[0]) % 2 == 1, ed_ref[0, at, :], ed_ref[1, at, :]
        )

    def build(into, p, r0):
        at = slice(CH + r0, CH + r0 + 128)
        for k in range(2):
            r = p + k * half
            mid = x_ref[r, at, :]
            edge = pltpu.roll(ed_ref[0, r0 : r0 + 128, :], 128 - 2 * (first + r), 1)
            into[k, 0, at, :] = jnp.where(lane == 0, edge, pltpu.roll(mid, 1, 1))
            into[k, 1, at, :] = jnp.where(lane == 127, edge, pltpu.roll(mid, 127, 1))

    fetch[0].wait()
    fetch[half].wait()
    for r0 in range(0, ROWS, 128):
        build(even_ref, 0, r0)
    weights.wait()
    fetch[half - 1].wait()

    def arrived(r):
        pltpu.make_async_copy(halo_ref, x_ref.at[r, body, :], sem.at[r]).wait()

    def out(row):
        return pltpu.make_async_copy(o_buf.at[row], o_ref.at[row], out_sem.at[row])

    def before(p):
        if p < half - 2:
            arrived(p + 1)
        if p < half - 1:
            arrived(p + 1 + half)
        if p > 2:
            out(p - 3).start()
            out(p + half - 3).start()

    def emit(row, at, value):
        same = x_ref[row + 1, CH + at.start : CH + at.stop, :].astype(F32)
        o_buf[row, at, :] = (value + same).astype(BF)

    def step(p, shifted, following):
        before(p)

        def cells(r0):
            rows = slice(r0, r0 + 256)
            sides = []
            for k in range(2):
                middle = x_ref[p + k * half, rows, :]
                sides.append(
                    jnp.concatenate(
                        [shifted[k, 0, rows, :], middle, shifted[k, 1, rows, :]], axis=0
                    )
                )
            return jnp.concatenate(sides, axis=1)

        def after(r0):
            if following is not None:
                build(following, p + 1, r0)

        band_step(p, half, w_buf, cells, a1_ref, a2_ref, s_ref, emit, after)

    for p in range(half):
        planes = (even_ref, odd_ref)
        step(p, planes[p % 2], planes[(p + 1) % 2] if p < half - 1 else None)
    band_seam(half, a1_ref, a2_ref, s_ref, emit)
    for row in (half - 3, 2 * half - 3, half - 2, half - 1):
        out(row).start()
    for row in range(8):
        out(row).wait()


def lift(part, where, band, field, halo, theirs, across):
    anywhere = pl.BlockSpec(memory_space=pl.ANY)
    return pl.pallas_call(
        functools.partial(lift_kernel, part),
        in_specs=[pl.BlockSpec(memory_space=pltpu.SMEM)] + [anywhere] * 5,
        out_specs=anywhere,
        out_shape=jax.ShapeDtypeStruct((8, ROWS, LANES), BF),
        scratch_shapes=[
            VMEM((384, 768), BF),
            VMEM((10, PADDED, LANES), BF),
            VMEM((2, 2, PADDED, LANES), BF),
            VMEM((2, 2, PADDED, LANES), BF),
        ]
        + conv_scratch()
        + [
            VMEM((2, ROWS, LANES), BF),
            VMEM((8, ROWS, LANES), BF),
            pltpu.SemaphoreType.DMA((10,)),
            pltpu.SemaphoreType.DMA((3,)),
            pltpu.SemaphoreType.DMA((8,)),
        ],
        compiler_params=params(60),
        cost_estimate=cost(8e9, 8e6),
        name="lift",
    )(where, band, field, halo, theirs, across)


def split(x):
    high = x.astype(BF)
    return high, (x - high.astype(F32)).astype(BF)


def mix_kernel(p_ref, re_ref, im_ref, o_ref):
    total = p_ref[0].astype(F32)
    for i in range(1, 16):
        total = total + p_ref[i].astype(F32)
    both = jnp.concatenate([total[0:CH], total[CH : 2 * CH]], axis=1)
    lane = lax.broadcasted_iota(jnp.int32, (CH, 256), 1)
    is_re = lane % 32 < MODES
    turned = jnp.where(is_re, -pltpu.roll(both, 256 - MODES, 1), pltpu.roll(both, MODES, 1))
    bh, bl = split(both)
    th, tl = split(turned)
    dot = functools.partial(jnp.dot, preferred_element_type=F32)
    rh, rl = split(re_ref[...].reshape(MODES * CH, CH))
    ih, il = split(im_ref[...].reshape(MODES * CH, CH))
    high = jnp.concatenate([rh, ih], axis=1)
    low = jnp.concatenate([rl, il], axis=1)
    cells = jnp.concatenate([bh, th], axis=0)
    rest = jnp.concatenate([bl, tl], axis=0)
    every = dot(
        jnp.concatenate([high, low], axis=1), jnp.concatenate([cells, cells], axis=0)
    ) + dot(high, rest)
    mode = lane % MODES
    out = every[0:CH]
    for k in range(1, MODES):
        out = jnp.where(mode == k, every[k * CH : k * CH + CH], out)
    piece = jnp.concatenate([out[:, 0:128], out[:, 128:256]], axis=0).astype(BF)
    for i in range(16):
        o_ref[i] = piece


def mix(pieces, spec_re, spec_im):
    return pl.pallas_call(
        mix_kernel,
        out_shape=jax.ShapeDtypeStruct((16, 128, LANES), BF),
        compiler_params=params(16),
        cost_estimate=cost(5e8, 1e6),
        name="mix",
    )(pieces, spec_re, spec_im)


GELU_ONE = math.sqrt(2.0 / math.pi)
GELU_THREE = GELU_ONE * 0.044715


def finish_kernel(h_ref, la_ref, lb_ref, m_ref, inv_ref, up_ref, down_ref, *rest):
    o_ref, tab_ref, up_buf = rest[-3:]

    @pl.when(pl.program_id(0) == 0)
    def _():
        up_buf[...] = jnp.transpose(up_ref[...].astype(F32)).astype(BF)
        row = lax.broadcasted_iota(jnp.int32, (256, LANES), 0)
        inv = inv_ref[0]
        for g in range(4):
            tab_ref[:, g * 128 : g * 128 + 128] = jnp.where(
                (row // 32) % 4 == g, inv, jnp.zeros_like(inv)
            )

    dot = functools.partial(jnp.dot, preferred_element_type=F32)
    m = m_ref[0]
    branch = dot(jnp.concatenate([m, m], axis=1), tab_ref[...])
    lifted = jnp.concatenate([ref[g, 0] for ref in (la_ref, lb_ref) for g in range(2)], axis=1)
    blended = (lifted.astype(F32) + branch).astype(BF)
    cells = jnp.concatenate(
        [blended[z * CH : z * CH + CH] for z in range(CHUNK // CH)], axis=1
    )
    half_down = (0.5 * down_ref[...].astype(F32)).astype(BF)
    x = dot(up_buf[...], cells)
    bend = jnp.tanh(x * (GELU_ONE + GELU_THREE * (x * x)))
    hidden = (x * bend + x).astype(BF)
    out = cells.astype(F32) + dot(half_down, hidden)
    for z in range(CHUNK // CH):
        for g in range(4):
            c = (z * 4 + g) * 128
            o_ref[g, 0, z * CH : z * CH + CH, :] = out[:, c : c + 128].astype(BF)


def finish(half_at, where, first, last, mixed, inverse, mlp_in, mlp_out, into=None):
    chunks = ROWS // CHUNK
    layer = lambda s, h: (0, 2 * h[half_at] + s // chunks, s % chunks, 0)
    fixed = lambda *shape: pl.BlockSpec(shape, lambda s, h: (0,) * len(shape))
    operands = [where, first, last, mixed, inverse, mlp_in.T, mlp_out]
    specs = [
        pl.BlockSpec((2, 1, CHUNK, LANES), layer),
        pl.BlockSpec((2, 1, CHUNK, LANES), layer),
        pl.BlockSpec((1, CHUNK, LANES), lambda s, h: (s // chunks, s % chunks, 0)),
        pl.BlockSpec((1, 256, LANES), lambda s, h: (h[1], 0, 0)),
        fixed(CH, HID),
        fixed(CH, HID),
    ]
    if into is not None:
        operands.append(into)
        specs.append(pl.BlockSpec(memory_space=pltpu.HBM))
    return pl.pallas_call(
        finish_kernel,
        grid_spec=pltpu.PrefetchScalarGridSpec(
            num_scalar_prefetch=1,
            grid=(2 * chunks,),
            in_specs=specs,
            out_specs=pl.BlockSpec((4, 1, CHUNK, LANES), layer),
            scratch_shapes=[VMEM((256, 512), BF), VMEM((HID, CH), BF)],
        ),
        out_shape=jax.ShapeDtypeStruct((4, 4, ROWS, LANES), BF),
        input_output_aliases={} if into is None else {7: 0},
        compiler_params=params(52),
        cost_estimate=cost(5e9, 6e6),
        name="finish",
    )(*operands)


def per_device(forward, inverse, field, conv_w, spec_re, spec_im, mlp_in, mlp_out):
    rows_y, depth, channels, width = field.shape
    blocks, layers = lax.axis_size("gx"), lax.axis_size("gy")
    place = lax.axis_index("gx")
    core = place % 2
    f = field.reshape(rows_y, depth * channels, width)

    up_y = [(i, i + 1) for i in range(layers - 1)]
    down_y = [(j, i) for i, j in up_y]
    neighbour = [(i, i + 1) for i in range(1, blocks - 1, 2)]
    neighbour = neighbour + [(j, i) for i, j in neighbour]
    partner = [(i, i ^ 1) for i in range(blocks)]
    chips = [[i for i in range(c, blocks, 2)] for c in range(2)]

    top = lax.ppermute(f[rows_y - 1], "gy", up_y)
    bottom = lax.ppermute(f[0], "gy", down_y)
    where = jnp.stack([core, place, 1 - core]).astype(jnp.int32)
    table = lax.dynamic_index_in_dim(forward, place, 0, keepdims=False)
    modes, own, edges, band = dft(f, table, conv_w)
    above, below, edges = halo_modes(top, bottom, table, edges)
    across = lax.ppermute(edges, "gx", neighbour)
    mine, other = spectral(where, band, modes, own, above, below, edges)
    other, across = lax.optimization_barrier((other, across))
    theirs = lax.ppermute(other, "gx", partner)
    chip_sum = add(mine, theirs)
    pieces = lax.all_to_all(
        chip_sum.reshape(16, 128, LANES), "gx", 0, 0, axis_index_groups=chips, tiled=True
    )
    first = lift(0, where, band, f, top, theirs, across)
    pieces, first = lax.optimization_barrier((pieces, first))
    copies = mix(pieces, spec_re, spec_im)
    mixed = lax.all_to_all(copies, "gx", 0, 0, axis_index_groups=chips, tiled=True)
    last = lift(1, where, band, f, bottom, theirs, across)
    mixed, last = lax.optimization_barrier((mixed, last))
    mixed = mixed.reshape(2, ROWS, LANES)
    mixed_other = lax.ppermute(mixed, "gx", partner)
    first = first.reshape(2, 4, ROWS, LANES)
    last = last.reshape(2, 4, ROWS, LANES)
    result = finish(0, where, first, last, mixed, inverse, mlp_in, mlp_out)
    result = finish(2, where, first, last, mixed_other, inverse, mlp_in, mlp_out, result)
    return result.reshape(field.shape)


def solution(mesh):
    in_specs = (P("gy", None, None, "gx"), P(), P(), P(), P(), P())
    out_specs = P("gy", None, None, "gx")
    forward, inverse = tables(mesh.shape["gx"], LANES)
    return jax.shard_map(
        functools.partial(per_device, jnp.asarray(forward), jnp.asarray(inverse)),
        mesh=mesh, in_specs=in_specs, out_specs=out_specs, check_vma=False,
    )
```
